32 devices in a mesh: section: 4 (over z), dp: 8 (over y, x, core).
Axes of the slice: x: 2, y: 2, z: 4, core: 2. Of those that a mesh axis runs over, the one named last changes fastest.
Arguments:
- x_in: bfloat16 [8, 4, 128, 768], P('dp'), may hold values from -8 to 8
- cotangent: bfloat16 [8, 4, 128, 768], P('dp'), may hold values from -0.15625 to 0.15625
- w_in: bfloat16 [4, 768, 3072], P('section'), may hold values from -0.21875 to 0.21875
- w_out: bfloat16 [4, 768, 3072], P('section'), may hold values from -0.109375 to 0.109375
- gain: bfloat16 [4, 768], P('section'), may hold values from 0.099609375 to 1.8984375
- drop_mask: int32 [8, 4, 1, 4], P('dp'), may hold values 0 or 1
Outputs:
- grad_in: float32 [4, 768, 3072], P('section', 'dp')
- grad_out: float32 [4, 768, 3072], P('section', 'dp')
- grad_gain: float32 [4, 768], P('section', 'dp')
The draws below stay inside these ranges and needn't reach their ends.
All inputs are finite; a program needn't handle non-finite values. No bound on the sum of `drop_mask` on one device may be relied on, other than what follows from the above.
Results may differ from the reference program's by a relative error of at most 0.035.
Values may be sent and summed in bfloat16 or wider, within the bound.
A program may use at most 256 MiB of HBM per device.

```python
import jax
import jax.numpy as jnp
from jax import lax

D = 768
HID = 3072
SEQ = 128
MICRO = 4
MB_SEQS = 1
ROWS = 128
LAYERS = 4
REPLICAS = 8


def set_ends(values, stream_key, smallest, largest):
    shape = values.shape
    place = [jax.random.randint(jax.random.fold_in(stream_key, axis), (), 0, shape[axis]) for axis in range(len(shape))]
    values = values.at[tuple(place)].set(smallest)
    longest = shape.index(max(shape))
    place[longest] = (place[longest] + 1) % shape[longest]
    return values.at[tuple(place)].set(largest)


def raised(values, stream_key, source, target, blocks, factor):
    def block_of(dim):
        return (jnp.arange(values.shape[dim]) // (values.shape[dim] // blocks)).reshape((-1,) + (1,) * (values.ndim - 1 - dim))

    first = jax.random.permutation(stream_key, blocks)[block_of(target)]
    other_side = (block_of(target) + blocks // 2) % blocks
    return jnp.where((block_of(source) == first) | (block_of(source) == other_side), factor * values, values)


def shard_levels(own_key, extent, cuts, least, high):
    level = 1.0
    for axis_at, shards_of in cuts:
        steps = jax.random.uniform(jax.random.fold_in(jax.random.fold_in(own_key, 6), axis_at), (shards_of,), jnp.float32, least / len(cuts), high / len(cuts))
        level = level * jnp.repeat(jnp.exp(steps), extent[axis_at] // shards_of).reshape((-1,) + (1,) * (len(extent) - 1 - axis_at))
    return level


def scatter_about(key, dims, scale, bound, cuts=(), dtype=jnp.bfloat16):
    array = scale * jax.random.normal(key, dims, jnp.float32)
    if cuts:
        array = array * shard_levels(key, dims, cuts, -0.22, 0.18)
    return jnp.clip(array, -bound, bound).astype(dtype)


def bell_draw_with(key, shape, spread, limit, shards, heavy, kind=jnp.bfloat16):
    result = spread * jax.random.normal(key, shape, jnp.float32)
    if shards:
        result = result * shard_levels(key, shape, shards, -0.22, 0.18)
    return jnp.clip(raised(result, jax.random.fold_in(key, 3), *heavy), -limit, limit).astype(kind)


def setup_inputs(seed: int = 0) -> dict:
    splits = jax.random.split(jax.random.key(seed), 7)
    x_in = bell_draw_with(splits[0], (REPLICAS, MICRO, ROWS, D), 1.0, 8.0, ((0, 8),), (0, 3, 8, 2.0))
    cotangent = bell_draw_with(splits[1], (REPLICAS, MICRO, ROWS, D), 0.02, 0.15625, ((0, 8),), (0, 3, 8, 2.0))
    w_in = scatter_about(splits[2], (LAYERS, D, HID), D ** -0.5, 0.21875, ((0, 4),))
    w_out = scatter_about(splits[3], (LAYERS, D, HID), HID ** -0.5, 0.109375, ((0, 4),))
    gain = jnp.clip(1.0 + 0.18 * jax.random.normal(splits[4], (LAYERS, D), jnp.float32), 0.099609375, 1.8984375).astype(jnp.bfloat16)
    drop_mask = set_ends((jax.random.randint(splits[5], (REPLICAS, MICRO, MB_SEQS, LAYERS), 0, 4) < 3).astype(jnp.int32), jax.random.fold_in(splits[5], 1), 0, 1)
    return dict(x_in=x_in, cotangent=cotangent, w_in=w_in, w_out=w_out, gain=gain, drop_mask=drop_mask)


EPSILON = 1e-05
ROOT_HALF = 0.7071067811865476
DENSITY_SCALE = 0.3989422804014327

def gelu_exact(hidden):
    return 0.5 * hidden * (1.0 + lax.erf(hidden * ROOT_HALF))

def gelu_slope(hidden):
    return 0.5 * (1.0 + lax.erf(hidden * ROOT_HALF)) + hidden * jnp.exp(-0.5 * hidden * hidden) * DENSITY_SCALE

def block_forward(inputs, keep_rows, gain_row, w_first, w_second):
    as_float = inputs.astype(jnp.float32)
    inv_rms = lax.rsqrt(lax.optimization_barrier(jnp.mean(as_float * as_float, axis=-1, keepdims=True)) + EPSILON)
    normed = (as_float * inv_rms * gain_row.astype(jnp.float32)).astype(jnp.bfloat16)
    hidden = jnp.dot(normed, w_first, preferred_element_type=jnp.float32)
    active = gelu_exact(hidden).astype(jnp.bfloat16)
    branch = lax.dot_general(active, w_second, (((1,), (1,)), ((), ())), preferred_element_type=jnp.float32)
    outputs = (as_float + keep_rows[:, None] * branch).astype(jnp.bfloat16)
    return (outputs, normed, hidden, active, inv_rms)

def block_backward(upstream, inputs, keep_rows, gain_row, w_first, w_second, normed, hidden, active, inv_rms):
    up_float = upstream.astype(jnp.float32)
    gated = (keep_rows[:, None] * up_float).astype(jnp.bfloat16)
    grad_second = lax.dot_general(gated, active, (((0,), (0,)), ((), ())), preferred_element_type=jnp.float32)
    grad_active = jnp.dot(gated, w_second, preferred_element_type=jnp.float32)
    grad_hidden = (grad_active * gelu_slope(hidden)).astype(jnp.bfloat16)
    grad_first = lax.dot_general(normed, grad_hidden, (((0,), (0,)), ((), ())), preferred_element_type=jnp.float32)
    grad_normed = lax.dot_general(grad_hidden, w_first, (((1,), (1,)), ((), ())), preferred_element_type=jnp.float32)
    as_float = inputs.astype(jnp.float32)
    grad_gain = lax.optimization_barrier(jnp.sum(grad_normed * as_float * inv_rms, axis=0))
    scaled_grad = grad_normed * gain_row.astype(jnp.float32)
    centre = lax.optimization_barrier(jnp.mean(scaled_grad * as_float, axis=-1, keepdims=True))
    grad_inputs = up_float + inv_rms * (scaled_grad - as_float * inv_rms * inv_rms * centre)
    return (grad_inputs.astype(jnp.bfloat16), grad_first, grad_second, grad_gain)

def one_half(rows_in, rows_cot, keep_rows, w_in, w_out, gain):
    layers = w_in.shape[0]
    carried = rows_in
    saved_parts = []
    for layer_index in range(layers):
        outputs, normed, hidden, active, inv_rms = block_forward(carried, keep_rows[:, layer_index], gain[layer_index], w_in[layer_index], w_out[layer_index])
        saved_parts.append((carried, normed, hidden, active, inv_rms))
        carried = lax.optimization_barrier(outputs)
    upstream = rows_cot
    firsts = [None] * layers
    seconds = [None] * layers
    gains = [None] * layers
    for layer_index in range(layers - 1, -1, -1):
        inputs, normed, hidden, active, inv_rms = saved_parts[layer_index]
        grad_inputs, grad_first, grad_second, grad_gain = block_backward(upstream, inputs, keep_rows[:, layer_index], gain[layer_index], w_in[layer_index], w_out[layer_index], normed, hidden, active, inv_rms)
        firsts[layer_index] = grad_first
        seconds[layer_index] = grad_second
        gains[layer_index] = grad_gain
        upstream = lax.optimization_barrier(grad_inputs)
    return (jnp.stack(firsts), jnp.stack(seconds), jnp.stack(gains))

def rounded(value_sum):
    return lax.optimization_barrier(value_sum.astype(jnp.bfloat16)).astype(jnp.float32)

def reference(x_in, cotangent, w_in, w_out, gain, drop_mask):
    half_count = MICRO // 2
    model_width = w_in.shape[1]

    def replica(totals, replica_items):
        inputs, cot_rows, drop_marks = replica_items
        keep_table = jnp.repeat(drop_marks.astype(jnp.float32), SEQ, axis=1)
        halves = []
        for portion in range(2):
            start = portion * half_count
            rows_in = inputs[start:start + half_count].reshape(-1, model_width)
            rows_cot = cot_rows[start:start + half_count].reshape(-1, model_width)
            keep_rows = keep_table[start:start + half_count].reshape(rows_in.shape[0], -1)
            halves.append(one_half(rows_in, rows_cot, keep_rows, w_in, w_out, gain))
        parts = tuple((rounded(rounded(first) + rounded(second)) for first, second in zip(halves[0], halves[1])))
        totals = tuple((total + part for total, part in zip(totals, parts)))
        return (totals, None)
    zero_sums = (jnp.zeros(w_in.shape, jnp.float32), jnp.zeros(w_out.shape, jnp.float32), jnp.zeros(gain.shape, jnp.float32))
    totals, unused = lax.scan(replica, zero_sums, (x_in, cotangent, drop_mask))
    return (totals[0], totals[1], totals[2])
```

```python
import functools

import jax
import jax.numpy as jnp
from jax import lax
from jax.experimental import pallas as pl
from jax.experimental.pallas import tpu as pltpu
from jax.sharding import PartitionSpec as P

EPSILON = 1e-05
ROOT_HALF = 0.7071067811865476
DENSITY_SCALE = 0.3989422804014327
MESH = pl.DeviceIdType.MESH

CHUNK_ROWS = 64
LAG = 2
HIDDEN_BLOCK = 512
TILE = 512
TRANSPOSED_RHS = (((1,), (1,)), ((), ()))


def largest_divisor(extent, limit, step):
    best = extent
    for size in range(step, min(extent, limit) + 1, step):
        if extent % size == 0:
            best = size
    return best


def position(block, order):
    place = 0
    for bit in order:
        place = 2 * place + ((block >> bit) & 1)
    return place


def kernel(
    dims, keep_ref, gain_ref, x_hbm, cot_hbm, w1_hbm, w2_hbm, grad_in_ref, grad_out_ref, grad_gain_ref,
    w1, w2, h_in, g_in, h_out, g_out, normed_all, gated_all, active_all, slope_all, hidden_grad_all,
    gain_sum, normed_t, gated_t, parts_a, parts_b, parts_g, *rest,
):
    sections, shards, chunk, chunks, seq_len, block, tile, tiles, steps = dims
    landed_a, landed_b, landed_g = rest[:steps], rest[steps : 2 * steps], rest[2 * steps : 3 * steps]
    (load_sem, h_send, h_recv, g_send, g_recv, a_send, a_recv, b_send, b_recv, e_send, e_recv) = rest[3 * steps :]
    width, hidden_width = w1.shape
    section = lax.axis_index("section")
    shard = lax.axis_index("dp")
    first, last = section == 0, section == sections - 1
    bits = [lax.rem(shard // (1 << b), 2) for b in range(steps)]
    partners = [shard + (1 - 2 * bits[b]) * (1 << b) for b in range(steps)]

    loads = [
        pltpu.make_async_copy(w1_hbm, w1, load_sem.at[0]),
        pltpu.make_async_copy(w2_hbm, w2, load_sem.at[1]),
    ]
    entry = pltpu.make_async_copy(x_hbm, h_in, load_sem.at[2])
    cotangents = pltpu.make_async_copy(cot_hbm, g_in, load_sem.at[3])
    pl.when(first)(entry.start)
    for load in loads:
        load.start()
    pl.when(last)(cotangents.start)

    barrier = pltpu.get_barrier_semaphore()

    def greet(where):
        pl.semaphore_signal(barrier, inc=1, device_id=where, device_id_type=MESH)

    pl.when(section > 0)(lambda: greet({"section": section - 1}))
    pl.when(section < sections - 1)(lambda: greet({"section": section + 1}))
    for partner in partners:
        greet({"dp": partner})
    neighbours = jnp.where(first, 0, 1) + jnp.where(last, 0, 1)
    pl.semaphore_wait(barrier, steps + neighbours)

    def h_copy(index):
        return pltpu.make_async_remote_copy(
            h_out.at[index], h_in.at[index], h_send.at[index], h_recv.at[index],
            device_id={"section": section + 1}, device_id_type=MESH,
        )

    def g_copy(index):
        return pltpu.make_async_remote_copy(
            g_out.at[index], g_in.at[index], g_send.at[index], g_recv.at[index],
            device_id={"section": section - 1}, device_id_type=MESH,
        )

    gain_row = gain_ref[...].astype(jnp.float32)
    gain_sum[...] = jnp.zeros_like(gain_sum)
    column_blocks = [slice(at, at + block) for at in range(0, hidden_width, block)]

    def keep_of(index):
        return keep_ref[(index * chunk) // seq_len, section].astype(jnp.float32)

    def forward(index):
        pl.when(section > 0)(lambda: h_copy(index).wait_recv())
        rows = pl.ds(pl.multiple_of(index * chunk, chunk), chunk)
        inputs = h_in[index].astype(jnp.float32)
        inv_rms = lax.rsqrt(jnp.mean(inputs * inputs, axis=-1, keepdims=True) + EPSILON)
        normed = (inputs * inv_rms * gain_row).astype(jnp.bfloat16)
        normed_all[rows, :] = normed
        branch = jnp.zeros((chunk, width), jnp.float32)
        for columns in column_blocks:
            hidden = jnp.dot(normed, w1[:, columns], preferred_element_type=jnp.float32)
            share = 0.5 * (1.0 + lax.erf(hidden * ROOT_HALF))
            active = (hidden * share).astype(jnp.bfloat16)
            active_all[rows, columns] = active
            slope_all[rows, columns] = share + hidden * jnp.exp(-0.5 * hidden * hidden) * DENSITY_SCALE
            branch += lax.dot_general(
                active, w2[:, columns], TRANSPOSED_RHS, preferred_element_type=jnp.float32
            )

        @pl.when(section < sections - 1)
        def _():
            h_out[index] = (inputs + keep_of(index) * branch).astype(jnp.bfloat16)
            h_copy(index).start()

    def backward(index):
        pl.when(section < sections - 1)(lambda: g_copy(index).wait_recv())
        rows = pl.ds(pl.multiple_of(index * chunk, chunk), chunk)
        inputs = h_in[index].astype(jnp.float32)
        inv_rms = lax.rsqrt(jnp.mean(inputs * inputs, axis=-1, keepdims=True) + EPSILON)
        upstream = g_in[index].astype(jnp.float32)
        gated = (keep_of(index) * upstream).astype(jnp.bfloat16)
        gated_all[rows, :] = gated
        grad_normed = jnp.zeros((chunk, width), jnp.float32)
        for columns in column_blocks:
            grad_active = jnp.dot(gated, w2[:, columns], preferred_element_type=jnp.float32)
            grad_hidden = (grad_active * slope_all[rows, columns]).astype(jnp.bfloat16)
            hidden_grad_all[rows, columns] = grad_hidden
            grad_normed += lax.dot_general(
                grad_hidden, w1[:, columns], TRANSPOSED_RHS, preferred_element_type=jnp.float32
            )
        gain_sum[0:1, :] += jnp.sum(grad_normed * inputs * inv_rms, axis=0, keepdims=True)

        @pl.when(section > 0)
        def _():
            scaled = grad_normed * gain_row
            centre = jnp.mean(scaled * inputs, axis=-1, keepdims=True)
            grads = upstream + inv_rms * (scaled - inputs * inv_rms * inv_rms * centre)
            g_out[index] = grads.astype(jnp.bfloat16)
            g_copy(index).start()

    pl.when(first)(entry.wait)
    for load in loads:
        load.wait()
    pl.when(last)(cotangents.wait)

    def tick(moment, carry):
        ahead = moment - LAG * section
        behind = moment - LAG * (2 * (sections - 1) - section)
        pl.when(jnp.logical_and(ahead >= 0, ahead < chunks))(lambda: forward(ahead))
        pl.when(jnp.logical_and(behind >= 0, behind < chunks))(lambda: backward(behind))
        return carry

    lax.fori_loop(0, chunks + 2 * LAG * (sections - 1), tick, 0)

    upwards = list(range(steps))
    downwards = upwards[:1] + upwards[:0:-1]
    block_rows = width // shards

    def halving(order, parts, landed, send_sem, recv_sem):
        def copy(at, step):
            half = shards >> (step + 1)
            bit = order[step]
            source = parts if step == 0 else landed[step - 1]
            return pltpu.make_async_remote_copy(
                source.at[at, pl.ds((1 - bits[bit]) * half, half)],
                landed[step].at[at],
                send_sem.at[at, step],
                recv_sem.at[at, step],
                device_id={"dp": partners[bit]},
                device_id_type=MESH,
            )

        def fill(at, value):
            for shard_at in range(shards):
                rows = value[shard_at * block_rows : (shard_at + 1) * block_rows]
                parts[at, position(shard_at, order)] = rows.astype(jnp.bfloat16)
            copy(at, 0).start()

        def advance(at, step, finish):
            copy(at, step).wait_recv()
            half = shards >> (step + 1)
            source = parts if step == 0 else landed[step - 1]
            own = source[at, pl.ds(bits[order[step]] * half, half)].astype(jnp.float32)
            total = own + landed[step][at].astype(jnp.float32)
            if step + 1 < steps:
                landed[step][at] = total.astype(jnp.bfloat16)
                copy(at, step + 1).start()
            else:
                finish(total[0])

        def close(at):
            for step in range(steps):
                copy(at, step).wait_send()

        return fill, advance, close

    fill_a, advance_a, close_a = halving(upwards, parts_a, landed_a, a_send, a_recv)
    fill_b, advance_b, close_b = halving(downwards, parts_b, landed_b, b_send, b_recv)
    fill_g, advance_g, close_g = halving(upwards, parts_g, landed_g, e_send, e_recv)

    normed_t[...] = normed_all[...].T
    gated_t[...] = gated_all[...].T
    gain_lanes = jnp.broadcast_to(gain_sum[0:1, :], (128, width)).T

    def finish_gain(total):
        grad_gain_ref[...] = jnp.transpose(total)[0:1, :]

    def turn(moment, carry):
        @pl.when(moment < tiles)
        def _():
            columns = pl.ds(pl.multiple_of(moment * tile, tile), tile)
            fill_a(
                moment,
                jnp.dot(normed_t[...], hidden_grad_all[:, columns], preferred_element_type=jnp.float32),
            )
            fill_b(
                moment, jnp.dot(gated_t[...], active_all[:, columns], preferred_element_type=jnp.float32)
            )

        for step in range(steps):
            at = moment - (step + 1)

            @pl.when(jnp.logical_and(at >= 0, at < tiles))
            def _(at=at, step=step):
                columns = pl.ds(pl.multiple_of(at * tile, tile), tile)

                def finish_a(total):
                    grad_in_ref[:, columns] = total

                def finish_b(total):
                    grad_out_ref[:, columns] = total

                advance_a(at, step, finish_a)
                advance_b(at, step, finish_b)

            pl.when(moment == step + 2)(lambda step=step: advance_g(0, step, finish_gain))
        return carry

    fill_g(0, gain_lanes)
    lax.fori_loop(0, max(tiles, 2) + steps, turn, 0)

    def close_chunk(index, carry):
        pl.when(section < sections - 1)(lambda: h_copy(index).wait_send())
        pl.when(section > 0)(lambda: g_copy(index).wait_send())
        return carry

    lax.fori_loop(0, chunks, close_chunk, 0)

    def close_tile(at, carry):
        close_a(at)
        close_b(at)
        return carry

    lax.fori_loop(0, tiles, close_tile, 0)
    close_g(0)


def per_device(x_in, cotangent, w_in, w_out, gain, drop_mask):
    sections = lax.axis_size("section")
    shards = lax.axis_size("dp")
    micro, micro_rows, width = x_in.shape[1:]
    hidden_width = w_in.shape[2]
    samples, layers = drop_mask.shape[2:]
    seq_len = micro_rows // samples
    rows = micro * micro_rows
    chunk = largest_divisor(seq_len, CHUNK_ROWS, 16)
    chunks = rows // chunk
    block = largest_divisor(hidden_width, HIDDEN_BLOCK, 128)
    tile = largest_divisor(hidden_width, TILE, 128)
    tiles = hidden_width // tile
    steps = shards.bit_length() - 1
    assert shards == 1 << steps and steps >= 1
    block_rows = width // shards
    dims = (sections, shards, chunk, chunks, seq_len, block, tile, tiles, steps)

    def landing(count, columns):
        return [
            pltpu.VMEM((count, shards >> (step + 1), block_rows, columns), jnp.bfloat16)
            for step in range(steps)
        ]

    chunk_shape = (chunks, chunk, width)
    any_spec = pl.BlockSpec(memory_space=pl.ANY)
    vmem_spec = pl.BlockSpec(memory_space=pltpu.VMEM)
    dma = pltpu.SemaphoreType.DMA
    macs = 6 * rows * width * hidden_width
    grad_in, grad_out, grad_gain = pl.pallas_call(
        functools.partial(kernel, dims),
        out_shape=(
            jax.ShapeDtypeStruct((block_rows, hidden_width), jnp.float32),
            jax.ShapeDtypeStruct((block_rows, hidden_width), jnp.float32),
            jax.ShapeDtypeStruct((1, block_rows), jnp.float32),
        ),
        in_specs=[pl.BlockSpec(memory_space=pltpu.SMEM), vmem_spec] + [any_spec] * 4,
        out_specs=(vmem_spec,) * 3,
        scratch_shapes=[
            pltpu.VMEM((width, hidden_width), jnp.bfloat16),
            pltpu.VMEM((width, hidden_width), jnp.bfloat16),
            *[pltpu.VMEM(chunk_shape, jnp.bfloat16) for _ in range(4)],
            pltpu.VMEM((rows, width), jnp.bfloat16),
            pltpu.VMEM((rows, width), jnp.bfloat16),
            pltpu.VMEM((rows, hidden_width), jnp.bfloat16),
            pltpu.VMEM((rows, hidden_width), jnp.float32),
            pltpu.VMEM((rows, hidden_width), jnp.bfloat16),
            pltpu.VMEM((8, width), jnp.float32),
            pltpu.VMEM((width, rows), jnp.bfloat16),
            pltpu.VMEM((width, rows), jnp.bfloat16),
            pltpu.VMEM((tiles, shards, block_rows, tile), jnp.bfloat16),
            pltpu.VMEM((tiles, shards, block_rows, tile), jnp.bfloat16),
            pltpu.VMEM((1, shards, block_rows, 128), jnp.bfloat16),
            *landing(tiles, tile),
            *landing(tiles, tile),
            *landing(1, 128),
            dma((4,)),
            *[dma((chunks,)) for _ in range(4)],
            *[dma((tiles, steps)) for _ in range(4)],
            *[dma((1, steps)) for _ in range(2)],
        ],
        compiler_params=pltpu.CompilerParams(
            collective_id=0, has_side_effects=True, vmem_limit_bytes=62 * 1024 * 1024
        ),
        cost_estimate=pl.CostEstimate(
            flops=2 * macs, bytes_accessed=8 * width * hidden_width, transcendentals=2 * rows * hidden_width
        ),
        name="window",
    )(
        drop_mask[0].reshape(micro * samples, layers),
        gain,
        x_in[0].reshape(chunk_shape),
        cotangent[0].reshape(chunk_shape),
        w_in[0],
        w_out[0],
    )
    return (grad_in[None], grad_out[None], grad_gain)


def solution(mesh):
    placed = (
        P("dp", None, None, None),
        P("dp", None, None, None),
        P("section", None, None),
        P("section", None, None),
        P("section", None),
        P("dp", None, None, None),
    )
    return jax.shard_map(
        per_device,
        mesh=mesh,
        in_specs=placed,
        out_specs=(P("section", "dp", None), P("section", "dp", None), P("section", "dp")),
        check_vma=False,
    )
```

```python
import functools

import jax
import jax.numpy as jnp
from jax import lax
from jax.experimental import pallas as pl
from jax.experimental.pallas import tpu as pltpu
from jax.sharding import PartitionSpec as P

EPSILON = 1e-05
ROOT_HALF = 0.7071067811865476
DENSITY_SCALE = 0.3989422804014327
MESH = pl.DeviceIdType.MESH

CHUNK_ROWS = 64
LAG = 3
HIDDEN_BLOCK = 512
TILE = 256
TRANSPOSED_RHS = (((1,), (1,)), ((), ()))


def largest_divisor(extent, limit, step):
    best = extent
    for size in range(step, min(extent, limit) + 1, step):
        if extent % size == 0:
            best = size
    return best


def position(block, order):
    place = 0
    for bit in order:
        place = 2 * place + ((block >> bit) & 1)
    return place


def kernel(
    dims, keep_ref, gain_ref, x_hbm, cot_hbm, w1_hbm, w2_hbm, grad_in_ref, grad_out_ref, grad_gain_ref,
    w1, w2, h_in, g_in, h_out, g_out, normed_all, gated_all, active_all, slope_all, hidden_grad_all,
    gain_sum, normed_t, gated_t, parts_a, parts_b, parts_g, *rest,
):
    sections, shards, chunk, chunks, seq_len, block, tile, tiles, steps = dims
    landed_a, landed_b, landed_g = rest[:steps], rest[steps : 2 * steps], rest[2 * steps : 3 * steps]
    (load_sem, h_send, h_recv, g_send, g_recv, a_send, a_recv, b_send, b_recv, e_send, e_recv) = rest[3 * steps :]
    width, hidden_width = w1.shape
    section = lax.axis_index("section")
    shard = lax.axis_index("dp")
    first, last = section == 0, section == sections - 1
    bits = [lax.rem(shard // (1 << b), 2) for b in range(steps)]
    partners = [shard + (1 - 2 * bits[b]) * (1 << b) for b in range(steps)]

    loads = [
        pltpu.make_async_copy(w1_hbm, w1, load_sem.at[0]),
        pltpu.make_async_copy(w2_hbm, w2, load_sem.at[1]),
    ]
    entry = pltpu.make_async_copy(x_hbm, h_in, load_sem.at[2])
    cotangents = pltpu.make_async_copy(cot_hbm, g_in, load_sem.at[3])
    pl.when(first)(entry.start)
    for load in loads:
        load.start()
    pl.when(last)(cotangents.start)

    barrier = pltpu.get_barrier_semaphore()

    def greet(where):
        pl.semaphore_signal(barrier, inc=1, device_id=where, device_id_type=MESH)

    pl.when(section > 0)(lambda: greet({"section": section - 1}))
    pl.when(section < sections - 1)(lambda: greet({"section": section + 1}))
    for partner in partners:
        greet({"dp": partner})
    neighbours = jnp.where(first, 0, 1) + jnp.where(last, 0, 1)
    pl.semaphore_wait(barrier, steps + neighbours)

    def h_copy(index):
        return pltpu.make_async_remote_copy(
            h_out.at[index], h_in.at[index], h_send.at[index], h_recv.at[index],
            device_id={"section": section + 1}, device_id_type=MESH,
        )

    def g_copy(index):
        return pltpu.make_async_remote_copy(
            g_out.at[index], g_in.at[index], g_send.at[index], g_recv.at[index],
            device_id={"section": section - 1}, device_id_type=MESH,
        )

    gain_row = gain_ref[...].astype(jnp.float32)
    gain_sum[...] = jnp.zeros_like(gain_sum)
    column_blocks = [slice(at, at + block) for at in range(0, hidden_width, block)]

    def keep_of(index):
        return keep_ref[(index * chunk) // seq_len, section].astype(jnp.float32)

    def forward(index):
        pl.when(section > 0)(lambda: h_copy(index).wait_recv())
        rows = pl.ds(pl.multiple_of(index * chunk, chunk), chunk)
        inputs = h_in[index].astype(jnp.float32)
        inv_rms = lax.rsqrt(jnp.mean(inputs * inputs, axis=-1, keepdims=True) + EPSILON)
        normed = (inputs * inv_rms * gain_row).astype(jnp.bfloat16)
        normed_all[rows, :] = normed
        branch = jnp.zeros((chunk, width), jnp.float32)
        for columns in column_blocks:
            hidden = jnp.dot(normed, w1[:, columns], preferred_element_type=jnp.float32)
            share = 0.5 * (1.0 + lax.erf(hidden * ROOT_HALF))
            active = (hidden * share).astype(jnp.bfloat16)
            active_all[rows, columns] = active
            slope_all[rows, columns] = share + hidden * jnp.exp(-0.5 * hidden * hidden) * DENSITY_SCALE
            branch += lax.dot_general(
                active, w2[:, columns], TRANSPOSED_RHS, preferred_element_type=jnp.float32
            )
        h_out[index] = (inputs + keep_of(index) * branch).astype(jnp.bfloat16)
        h_copy(index).start()

        @pl.when(index == chunks - 1)
        def _():
            normed_t[...] = normed_all[...].T

    def finish_chunk(index, inputs, inv_rms, upstream, grad_normed):
        @pl.when(section > 0)
        def _():
            scaled = grad_normed * gain_row
            centre = jnp.mean(scaled * inputs, axis=-1, keepdims=True)
            grads = upstream + inv_rms * (scaled - inputs * inv_rms * inv_rms * centre)
            g_out[index] = grads.astype(jnp.bfloat16)
            g_copy(index).start()

        gain_sum[0:1, :] += jnp.sum(grad_normed * inputs * inv_rms, axis=0, keepdims=True)

    def both(index):
        pl.when(section > 0)(lambda: h_copy(index).wait_recv())
        rows = pl.ds(pl.multiple_of(index * chunk, chunk), chunk)
        inputs = h_in[index].astype(jnp.float32)
        inv_rms = lax.rsqrt(jnp.mean(inputs * inputs, axis=-1, keepdims=True) + EPSILON)
        normed = (inputs * inv_rms * gain_row).astype(jnp.bfloat16)
        normed_all[rows, :] = normed
        upstream = g_in[index].astype(jnp.float32)
        gated = (keep_of(index) * upstream).astype(jnp.bfloat16)
        gated_all[rows, :] = gated
        grad_normed = jnp.zeros((chunk, width), jnp.float32)
        for columns in column_blocks:
            hidden = jnp.dot(normed, w1[:, columns], preferred_element_type=jnp.float32)
            grad_active = jnp.dot(gated, w2[:, columns], preferred_element_type=jnp.float32)
            share = 0.5 * (1.0 + lax.erf(hidden * ROOT_HALF))
            active_all[rows, columns] = (hidden * share).astype(jnp.bfloat16)
            slope = share + hidden * jnp.exp(-0.5 * hidden * hidden) * DENSITY_SCALE
            grad_hidden = (grad_active * slope).astype(jnp.bfloat16)
            hidden_grad_all[rows, columns] = grad_hidden
            grad_normed += lax.dot_general(
                grad_hidden, w1[:, columns], TRANSPOSED_RHS, preferred_element_type=jnp.float32
            )
        finish_chunk(index, inputs, inv_rms, upstream, grad_normed)

        @pl.when(index == chunks - 1)
        def _():
            normed_t[...] = normed_all[...].T

    def backward(index):
        g_copy(index).wait_recv()
        rows = pl.ds(pl.multiple_of(index * chunk, chunk), chunk)
        inputs = h_in[index].astype(jnp.float32)
        inv_rms = lax.rsqrt(jnp.mean(inputs * inputs, axis=-1, keepdims=True) + EPSILON)
        upstream = g_in[index].astype(jnp.float32)
        gated = (keep_of(index) * upstream).astype(jnp.bfloat16)
        gated_all[rows, :] = gated
        grad_normed = jnp.zeros((chunk, width), jnp.float32)
        for columns in column_blocks:
            grad_active = jnp.dot(gated, w2[:, columns], preferred_element_type=jnp.float32)
            grad_hidden = (grad_active * slope_all[rows, columns]).astype(jnp.bfloat16)
            hidden_grad_all[rows, columns] = grad_hidden
            grad_normed += lax.dot_general(
                grad_hidden, w1[:, columns], TRANSPOSED_RHS, preferred_element_type=jnp.float32
            )
        finish_chunk(index, inputs, inv_rms, upstream, grad_normed)

    pl.when(first)(entry.wait)
    for load in loads:
        load.wait()
    pl.when(last)(cotangents.wait)

    def tick(moment, carry):
        ahead = moment - LAG * section
        behind = moment - LAG * (2 * (sections - 1) - section)
        pl.when(jnp.logical_and(ahead >= 0, ahead < chunks))(lambda: forward(ahead))
        pl.when(jnp.logical_and(behind >= 0, behind < chunks))(lambda: backward(behind))
        return carry

    def last_tick(index, carry):
        both(index)
        return carry

    @pl.when(last)
    def _():
        lax.fori_loop(0, chunks, last_tick, 0)

    @pl.when(section < sections - 1)
    def _():
        lax.fori_loop(0, chunks + 2 * LAG * (sections - 1), tick, 0)

    upwards = list(range(steps))
    downwards = upwards[:1] + upwards[:0:-1]
    block_rows = width // shards

    def halving(order, parts, landed, send_sem, recv_sem):
        def copy(at, step):
            half = shards >> (step + 1)
            bit = order[step]
            source = parts if step == 0 else landed[step - 1]
            return pltpu.make_async_remote_copy(
                source.at[at, pl.ds((1 - bits[bit]) * half, half)],
                landed[step].at[at],
                send_sem.at[at, step],
                recv_sem.at[at, step],
                device_id={"dp": partners[bit]},
                device_id_type=MESH,
            )

        def fill(at, value):
            for shard_at in range(shards):
                rows = value[shard_at * block_rows : (shard_at + 1) * block_rows]
                parts[at, position(shard_at, order)] = rows.astype(jnp.bfloat16)
            copy(at, 0).start()

        def advance(at, step, finish):
            copy(at, step).wait_recv()
            half = shards >> (step + 1)
            source = parts if step == 0 else landed[step - 1]
            own = source[at, pl.ds(bits[order[step]] * half, half)].astype(jnp.float32)
            total = own + landed[step][at].astype(jnp.float32)
            if step + 1 < steps:
                landed[step][at] = total.astype(jnp.bfloat16)
                copy(at, step + 1).start()
            else:
                finish(total[0])

        def close(at):
            for step in range(steps):
                copy(at, step).wait_send()

        return fill, advance, close

    fill_a, advance_a, close_a = halving(upwards, parts_a, landed_a, a_send, a_recv)
    fill_b, advance_b, close_b = halving(downwards, parts_b, landed_b, b_send, b_recv)
    fill_g, advance_g, close_g = halving(upwards, parts_g, landed_g, e_send, e_recv)

    gated_t[...] = gated_all[...].T
    gain_lanes = jnp.broadcast_to(gain_sum[0:1, :], (128, width)).T

    def finish_gain(total):
        grad_gain_ref[...] = jnp.transpose(total)[0:1, :]

    def turn(moment, carry):
        @pl.when(moment < tiles)
        def _():
            columns = pl.ds(pl.multiple_of(moment * tile, tile), tile)
            fill_a(
                moment,
                jnp.dot(normed_t[...], hidden_grad_all[:, columns], preferred_element_type=jnp.float32),
            )
            fill_b(
                moment, jnp.dot(gated_t[...], active_all[:, columns], preferred_element_type=jnp.float32)
            )

        for step in range(steps):
            at = moment - (step + 1)

            @pl.when(jnp.logical_and(at >= 0, at < tiles))
            def _(at=at, step=step):
                columns = pl.ds(pl.multiple_of(at * tile, tile), tile)

                def finish_a(total):
                    grad_in_ref[:, columns] = total

                def finish_b(total):
                    grad_out_ref[:, columns] = total

                advance_a(at, step, finish_a)
                advance_b(at, step, finish_b)

            pl.when(moment == step + 2)(lambda step=step: advance_g(0, step, finish_gain))
        return carry

    fill_g(0, gain_lanes)
    lax.fori_loop(0, max(tiles, 2) + steps, turn, 0)

    def close_chunk(index, carry):
        pl.when(section < sections - 1)(lambda: h_copy(index).wait_send())
        pl.when(section > 0)(lambda: g_copy(index).wait_send())
        return carry

    lax.fori_loop(0, chunks, close_chunk, 0)

    def close_tile(at, carry):
        close_a(at)
        close_b(at)
        return carry

    lax.fori_loop(0, tiles, close_tile, 0)
    close_g(0)


def per_device(x_in, cotangent, w_in, w_out, gain, drop_mask):
    sections = lax.axis_size("section")
    shards = lax.axis_size("dp")
    micro, micro_rows, width = x_in.shape[1:]
    hidden_width = w_in.shape[2]
    samples, layers = drop_mask.shape[2:]
    seq_len = micro_rows // samples
    rows = micro * micro_rows
    chunk = largest_divisor(seq_len, CHUNK_ROWS, 16)
    chunks = rows // chunk
    block = largest_divisor(hidden_width, HIDDEN_BLOCK, 128)
    tile = largest_divisor(hidden_width, TILE, 128)
    tiles = hidden_width // tile
    steps = shards.bit_length() - 1
    assert shards == 1 << steps and steps >= 1
    block_rows = width // shards
    dims = (sections, shards, chunk, chunks, seq_len, block, tile, tiles, steps)

    def landing(count, columns):
        return [
            pltpu.VMEM((count, shards >> (step + 1), block_rows, columns), jnp.bfloat16)
            for step in range(steps)
        ]

    chunk_shape = (chunks, chunk, width)
    any_spec = pl.BlockSpec(memory_space=pl.ANY)
    vmem_spec = pl.BlockSpec(memory_space=pltpu.VMEM)
    dma = pltpu.SemaphoreType.DMA
    macs = 6 * rows * width * hidden_width
    grad_in, grad_out, grad_gain = pl.pallas_call(
        functools.partial(kernel, dims),
        out_shape=(
            jax.ShapeDtypeStruct((block_rows, hidden_width), jnp.float32),
            jax.ShapeDtypeStruct((block_rows, hidden_width), jnp.float32),
            jax.ShapeDtypeStruct((1, block_rows), jnp.float32),
        ),
        in_specs=[pl.BlockSpec(memory_space=pltpu.SMEM), vmem_spec] + [any_spec] * 4,
        out_specs=(vmem_spec,) * 3,
        scratch_shapes=[
            pltpu.VMEM((width, hidden_width), jnp.bfloat16),
            pltpu.VMEM((width, hidden_width), jnp.bfloat16),
            *[pltpu.VMEM(chunk_shape, jnp.bfloat16) for _ in range(4)],
            pltpu.VMEM((rows, width), jnp.bfloat16),
            pltpu.VMEM((rows, width), jnp.bfloat16),
            pltpu.VMEM((rows, hidden_width), jnp.bfloat16),
            pltpu.VMEM((rows, hidden_width), jnp.float32),
            pltpu.VMEM((rows, hidden_width), jnp.bfloat16),
            pltpu.VMEM((8, width), jnp.float32),
            pltpu.VMEM((width, rows), jnp.bfloat16),
            pltpu.VMEM((width, rows), jnp.bfloat16),
            pltpu.VMEM((tiles, shards, block_rows, tile), jnp.bfloat16),
            pltpu.VMEM((tiles, shards, block_rows, tile), jnp.bfloat16),
            pltpu.VMEM((1, shards, block_rows, 128), jnp.bfloat16),
            *landing(tiles, tile),
            *landing(tiles, tile),
            *landing(1, 128),
            dma((4,)),
            *[dma((chunks,)) for _ in range(4)],
            *[dma((tiles, steps)) for _ in range(4)],
            *[dma((1, steps)) for _ in range(2)],
        ],
        compiler_params=pltpu.CompilerParams(
            collective_id=0, has_side_effects=True, vmem_limit_bytes=62 * 1024 * 1024
        ),
        cost_estimate=pl.CostEstimate(
            flops=2 * macs, bytes_accessed=8 * width * hidden_width, transcendentals=2 * rows * hidden_width
        ),
        name="window",
    )(
        drop_mask[0].reshape(micro * samples, layers),
        gain,
        x_in[0].reshape(chunk_shape),
        cotangent[0].reshape(chunk_shape),
        w_in[0],
        w_out[0],
    )
    return (grad_in[None], grad_out[None], grad_gain)


def solution(mesh):
    placed = (
        P("dp", None, None, None),
        P("dp", None, None, None),
        P("section", None, None),
        P("section", None, None),
        P("section", None),
        P("dp", None, None, None),
    )
    return jax.shard_map(
        per_device,
        mesh=mesh,
        in_specs=placed,
        out_specs=(P("section", "dp", None), P("section", "dp", None), P("section", "dp")),
        check_vma=False,
    )
```

```python
import functools

import jax
import jax.numpy as jnp
from jax import lax
from jax.experimental import pallas as pl
from jax.experimental.pallas import tpu as pltpu
from jax.sharding import PartitionSpec as P

EPSILON = 1e-05
ROOT_HALF = 0.7071067811865476
DENSITY_SCALE = 0.3989422804014327
MESH = pl.DeviceIdType.MESH

CHUNK_ROWS = 64
LAG = 3
HIDDEN_BLOCK = 512
TILE = 256
TRANSPOSED_RHS = (((1,), (1,)), ((), ()))


def largest_divisor(extent, limit, step):
    best = extent
    for size in range(step, min(extent, limit) + 1, step):
        if extent % size == 0:
            best = size
    return best


def position(block, order):
    place = 0
    for bit in order:
        place = 2 * place + ((block >> bit) & 1)
    return place


def kernel(
    dims, keep_ref, gain_ref, x_hbm, cot_hbm, w1_hbm, w2_hbm, grad_in_ref, grad_out_ref, grad_gain_ref,
    w1, w2, h_in, g_in, h_out, g_out, normed_all, gated_all, active_all, slope_all, hidden_grad_all,
    gain_sum, normed_t, active_far, gated_far, own_t, far_t, parts_a, parts_b, parts_g, *rest,
):
    sections, shards, chunk, chunks, seq_len, block, tile, tiles, steps = dims
    landed_a = rest[:steps]
    landed_b = rest[steps : 2 * steps - 1]
    landed_g = rest[2 * steps - 1 : 3 * steps - 1]
    (load_sem, h_send, h_recv, g_send, g_recv, a_send, a_recv, b_send, b_recv, e_send, e_recv,
     active_send, active_recv, gated_send, gated_recv) = rest[3 * steps - 1 :]
    width, hidden_width = w1.shape
    section = lax.axis_index("section")
    shard = lax.axis_index("dp")
    first, last = section == 0, section == sections - 1
    bits = [lax.rem(shard // (1 << b), 2) for b in range(steps)]
    partners = [shard + (1 - 2 * bits[b]) * (1 << b) for b in range(steps)]

    loads = [
        pltpu.make_async_copy(w1_hbm, w1, load_sem.at[0]),
        pltpu.make_async_copy(w2_hbm, w2, load_sem.at[1]),
    ]
    entry = pltpu.make_async_copy(x_hbm, h_in, load_sem.at[2])
    cotangents = pltpu.make_async_copy(cot_hbm, g_in, load_sem.at[3])
    pl.when(first)(entry.start)
    for load in loads:
        load.start()
    pl.when(last)(cotangents.start)

    barrier = pltpu.get_barrier_semaphore()

    def greet(where):
        pl.semaphore_signal(barrier, inc=1, device_id=where, device_id_type=MESH)

    pl.when(section > 0)(lambda: greet({"section": section - 1}))
    pl.when(section < sections - 1)(lambda: greet({"section": section + 1}))
    for partner in partners:
        greet({"dp": partner})
    neighbours = jnp.where(first, 0, 1) + jnp.where(last, 0, 1)
    pl.semaphore_wait(barrier, steps + neighbours)

    def h_copy(index):
        return pltpu.make_async_remote_copy(
            h_out.at[index], h_in.at[index], h_send.at[index], h_recv.at[index],
            device_id={"section": section + 1}, device_id_type=MESH,
        )

    def g_copy(index):
        return pltpu.make_async_remote_copy(
            g_out.at[index], g_in.at[index], g_send.at[index], g_recv.at[index],
            device_id={"section": section - 1}, device_id_type=MESH,
        )

    pair_bits = (1, steps - 1)
    half_width = hidden_width // 2

    def active_copy(index, half):
        rows = pl.ds(pl.multiple_of(index * chunk, chunk), chunk)
        columns = slice(half * half_width, (half + 1) * half_width)
        return pltpu.make_async_remote_copy(
            active_all.at[rows, columns], active_far.at[rows, columns],
            active_send.at[index, half], active_recv.at[index, half],
            device_id={"dp": partners[pair_bits[half]]}, device_id_type=MESH,
        )

    def gated_copy(index, half):
        rows = pl.ds(pl.multiple_of(index * chunk, chunk), chunk)
        return pltpu.make_async_remote_copy(
            gated_all.at[rows], gated_far.at[half, rows],
            gated_send.at[index, half], gated_recv.at[index, half],
            device_id={"dp": partners[pair_bits[half]]}, device_id_type=MESH,
        )

    gain_row = gain_ref[...].astype(jnp.float32)
    gain_sum[...] = jnp.zeros_like(gain_sum)
    column_blocks = [slice(at, at + block) for at in range(0, hidden_width, block)]

    def keep_of(index):
        return keep_ref[(index * chunk) // seq_len, section].astype(jnp.float32)

    def forward(index):
        pl.when(section > 0)(lambda: h_copy(index).wait_recv())
        rows = pl.ds(pl.multiple_of(index * chunk, chunk), chunk)
        inputs = h_in[index].astype(jnp.float32)
        inv_rms = lax.rsqrt(jnp.mean(inputs * inputs, axis=-1, keepdims=True) + EPSILON)
        normed = (inputs * inv_rms * gain_row).astype(jnp.bfloat16)
        normed_all[rows, :] = normed
        branch = jnp.zeros((chunk, width), jnp.float32)
        for columns in column_blocks:
            hidden = jnp.dot(normed, w1[:, columns], preferred_element_type=jnp.float32)
            share = 0.5 * (1.0 + lax.erf(hidden * ROOT_HALF))
            active = (hidden * share).astype(jnp.bfloat16)
            active_all[rows, columns] = active
            slope_all[rows, columns] = share + hidden * jnp.exp(-0.5 * hidden * hidden) * DENSITY_SCALE
            branch += lax.dot_general(
                active, w2[:, columns], TRANSPOSED_RHS, preferred_element_type=jnp.float32
            )
        h_out[index] = (inputs + keep_of(index) * branch).astype(jnp.bfloat16)
        h_copy(index).start()
        for half in range(2):
            active_copy(index, half).start()

        @pl.when(index == chunks - 1)
        def _():
            normed_t[...] = normed_all[...].T

    def finish_chunk(index, inputs, inv_rms, upstream, grad_normed):
        @pl.when(section > 0)
        def _():
            scaled = grad_normed * gain_row
            centre = jnp.mean(scaled * inputs, axis=-1, keepdims=True)
            grads = upstream + inv_rms * (scaled - inputs * inv_rms * inv_rms * centre)
            g_out[index] = grads.astype(jnp.bfloat16)
            g_copy(index).start()

        gain_sum[0:1, :] += jnp.sum(grad_normed * inputs * inv_rms, axis=0, keepdims=True)

    def both(index):
        pl.when(section > 0)(lambda: h_copy(index).wait_recv())
        rows = pl.ds(pl.multiple_of(index * chunk, chunk), chunk)
        inputs = h_in[index].astype(jnp.float32)
        inv_rms = lax.rsqrt(jnp.mean(inputs * inputs, axis=-1, keepdims=True) + EPSILON)
        normed = (inputs * inv_rms * gain_row).astype(jnp.bfloat16)
        normed_all[rows, :] = normed
        upstream = g_in[index].astype(jnp.float32)
        gated = (keep_of(index) * upstream).astype(jnp.bfloat16)
        gated_all[rows, :] = gated
        for half in range(2):
            gated_copy(index, half).start()
        grad_normed = jnp.zeros((chunk, width), jnp.float32)
        for columns in column_blocks:
            hidden = jnp.dot(normed, w1[:, columns], preferred_element_type=jnp.float32)
            grad_active = jnp.dot(gated, w2[:, columns], preferred_element_type=jnp.float32)
            share = 0.5 * (1.0 + lax.erf(hidden * ROOT_HALF))
            active_all[rows, columns] = (hidden * share).astype(jnp.bfloat16)
            slope = share + hidden * jnp.exp(-0.5 * hidden * hidden) * DENSITY_SCALE
            grad_hidden = (grad_active * slope).astype(jnp.bfloat16)
            hidden_grad_all[rows, columns] = grad_hidden
            grad_normed += lax.dot_general(
                grad_hidden, w1[:, columns], TRANSPOSED_RHS, preferred_element_type=jnp.float32
            )
        for half in range(2):
            active_copy(index, half).start()
        finish_chunk(index, inputs, inv_rms, upstream, grad_normed)

        @pl.when(index == chunks - 1)
        def _():
            normed_t[...] = normed_all[...].T

    def backward(index):
        g_copy(index).wait_recv()
        rows = pl.ds(pl.multiple_of(index * chunk, chunk), chunk)
        inputs = h_in[index].astype(jnp.float32)
        inv_rms = lax.rsqrt(jnp.mean(inputs * inputs, axis=-1, keepdims=True) + EPSILON)
        upstream = g_in[index].astype(jnp.float32)
        gated = (keep_of(index) * upstream).astype(jnp.bfloat16)
        gated_all[rows, :] = gated
        for half in range(2):
            gated_copy(index, half).start()
        grad_normed = jnp.zeros((chunk, width), jnp.float32)
        for columns in column_blocks:
            grad_active = jnp.dot(gated, w2[:, columns], preferred_element_type=jnp.float32)
            grad_hidden = (grad_active * slope_all[rows, columns]).astype(jnp.bfloat16)
            hidden_grad_all[rows, columns] = grad_hidden
            grad_normed += lax.dot_general(
                grad_hidden, w1[:, columns], TRANSPOSED_RHS, preferred_element_type=jnp.float32
            )
        finish_chunk(index, inputs, inv_rms, upstream, grad_normed)

    pl.when(first)(entry.wait)
    for load in loads:
        load.wait()
    pl.when(last)(cotangents.wait)

    def tick(moment, carry):
        ahead = moment - LAG * section
        behind = moment - LAG * (2 * (sections - 1) - section)
        pl.when(jnp.logical_and(ahead >= 0, ahead < chunks))(lambda: forward(ahead))
        pl.when(jnp.logical_and(behind >= 0, behind < chunks))(lambda: backward(behind))
        return carry

    def last_tick(index, carry):
        both(index)
        return carry

    @pl.when(last)
    def _():
        lax.fori_loop(0, chunks, last_tick, 0)

    @pl.when(section < sections - 1)
    def _():
        lax.fori_loop(0, chunks + 2 * LAG * (sections - 1), tick, 0)

    orders_a = (list(range(steps)), [0] + list(range(steps - 1, 0, -1)))
    orders_b = tuple(
        [bit for bit in orders_a[1 - half] if bit != pair_bits[half]] for half in range(2)
    )
    block_rows = width // shards

    def halving(order, parts, landed, send_sem, recv_sem):
        count = 1 << len(order)

        def copy(at, step):
            half = count >> (step + 1)
            bit = order[step]
            source = parts if step == 0 else landed[step - 1]
            return pltpu.make_async_remote_copy(
                source.at[at, pl.ds((1 - bits[bit]) * half, half)],
                landed[step].at[at],
                send_sem.at[at, step],
                recv_sem.at[at, step],
                device_id={"dp": partners[bit]},
                device_id_type=MESH,
            )

        def fill(at, value, places):
            for number, place in enumerate(places):
                rows = value[number * block_rows : (number + 1) * block_rows]
                parts[at, place] = rows.astype(jnp.bfloat16)
            copy(at, 0).start()

        def advance(at, step, finish):
            copy(at, step).wait_recv()
            half = count >> (step + 1)
            source = parts if step == 0 else landed[step - 1]
            own = source[at, pl.ds(bits[order[step]] * half, half)].astype(jnp.float32)
            total = own + landed[step][at].astype(jnp.float32)
            if step + 1 < len(order):
                landed[step][at] = total.astype(jnp.bfloat16)
                copy(at, step + 1).start()
            else:
                finish(total[0])

        def close(at):
            for step in range(len(order)):
                copy(at, step).wait_send()

        return fill, advance, close

    streams_a = [halving(order, parts_a, landed_a, a_send, a_recv) for order in orders_a]
    streams_b = [halving(order, parts_b, landed_b, b_send, b_recv) for order in orders_b]
    fill_g, advance_g, close_g = halving(orders_a[0], parts_g, landed_g, e_send, e_recv)
    gain_lanes = jnp.broadcast_to(gain_sum[0:1, :], (128, width)).T

    def finish_gain(total):
        grad_gain_ref[...] = jnp.transpose(total)[0:1, :]

    def select_features(ref, half, rows_first):
        turned = rows_first.astype(jnp.float32).T
        bit, order = pair_bits[half], orders_b[half]
        for place in range(shards // 2):
            low = sum(((place >> (len(order) - 1 - k)) & 1) << b for k, b in enumerate(order))
            high = low + (1 << bit)
            pieces = [turned[b * block_rows : (b + 1) * block_rows] for b in (low, high)]
            chosen = jnp.where(bits[bit] == 1, pieces[1], pieces[0])
            ref[half, place * block_rows : (place + 1) * block_rows] = chosen.astype(jnp.bfloat16)

    def prepare_b():
        def arrive(index, carry):
            for half in range(2):
                active_copy(index, half).wait_recv()
                gated_copy(index, half).wait_recv()
            return carry

        lax.fori_loop(0, chunks, arrive, 0)
        for half in range(2):
            select_features(own_t, half, gated_all[...])
            select_features(far_t, half, gated_far[half])

    def columns_of(at, half):
        return pl.ds(pl.multiple_of(at * tile + half * half_width, tile), tile)

    def turn(moment, carry):
        @pl.when(moment < tiles)
        def _():
            for half in range(2):
                value = jnp.dot(
                    normed_t[...],
                    hidden_grad_all[:, columns_of(moment, half)],
                    preferred_element_type=jnp.float32,
                )
                places = [position(b, orders_a[half]) for b in range(shards)]
                streams_a[half][0](half * tiles + moment, value, places)
            pl.when(moment == 0)(prepare_b)
            for half in range(2):
                columns = columns_of(moment, half)
                value = jnp.dot(
                    own_t[half], active_all[:, columns], preferred_element_type=jnp.float32
                ) + jnp.dot(far_t[half], active_far[:, columns], preferred_element_type=jnp.float32)
                streams_b[half][0](half * tiles + moment, value, range(shards // 2))

        for step in range(steps):
            at = moment - (step + 1)

            @pl.when(jnp.logical_and(at >= 0, at < tiles))
            def _(at=at, step=step):
                def finish(out_ref, half):
                    def store(total):
                        out_ref[:, columns_of(at, half)] = total

                    return store

                for half in range(2):
                    streams_a[half][1](half * tiles + at, step, finish(grad_in_ref, half))
                if step + 1 < steps:
                    for half in range(2):
                        streams_b[half][1](half * tiles + at, step, finish(grad_out_ref, half))

            pl.when(moment == step + 2)(lambda step=step: advance_g(0, step, finish_gain))
        return carry

    fill_g(0, gain_lanes, [position(b, orders_a[0]) for b in range(shards)])
    lax.fori_loop(0, max(tiles, 2) + steps, turn, 0)

    def close_chunk(index, carry):
        pl.when(section < sections - 1)(lambda: h_copy(index).wait_send())
        pl.when(section > 0)(lambda: g_copy(index).wait_send())
        for half in range(2):
            active_copy(index, half).wait_send()
            gated_copy(index, half).wait_send()
        return carry

    lax.fori_loop(0, chunks, close_chunk, 0)

    def close_tile(at, carry):
        for half in range(2):
            streams_a[half][2](half * tiles + at)
            streams_b[half][2](half * tiles + at)
        return carry

    lax.fori_loop(0, tiles, close_tile, 0)
    close_g(0)


def per_device(x_in, cotangent, w_in, w_out, gain, drop_mask):
    sections = lax.axis_size("section")
    shards = lax.axis_size("dp")
    micro, micro_rows, width = x_in.shape[1:]
    hidden_width = w_in.shape[2]
    samples, layers = drop_mask.shape[2:]
    seq_len = micro_rows // samples
    rows = micro * micro_rows
    chunk = largest_divisor(seq_len, CHUNK_ROWS, 16)
    chunks = rows // chunk
    block = largest_divisor(hidden_width, HIDDEN_BLOCK, 128)
    tile = largest_divisor(hidden_width // 2, TILE, 128)
    tiles = hidden_width // 2 // tile
    steps = shards.bit_length() - 1
    assert shards == 1 << steps and steps >= 2
    block_rows = width // shards
    dims = (sections, shards, chunk, chunks, seq_len, block, tile, tiles, steps)

    def landing(count, start, columns):
        return [
            pltpu.VMEM((count, shards >> (step + 1), block_rows, columns), jnp.bfloat16)
            for step in range(start, steps)
        ]

    chunk_shape = (chunks, chunk, width)
    any_spec = pl.BlockSpec(memory_space=pl.ANY)
    vmem_spec = pl.BlockSpec(memory_space=pltpu.VMEM)
    dma = pltpu.SemaphoreType.DMA
    macs = 6 * rows * width * hidden_width
    grad_in, grad_out, grad_gain = pl.pallas_call(
        functools.partial(kernel, dims),
        out_shape=(
            jax.ShapeDtypeStruct((block_rows, hidden_width), jnp.float32),
            jax.ShapeDtypeStruct((block_rows, hidden_width), jnp.float32),
            jax.ShapeDtypeStruct((1, block_rows), jnp.float32),
        ),
        in_specs=[pl.BlockSpec(memory_space=pltpu.SMEM), vmem_spec] + [any_spec] * 4,
        out_specs=(vmem_spec,) * 3,
        scratch_shapes=[
            pltpu.VMEM((width, hidden_width), jnp.bfloat16),
            pltpu.VMEM((width, hidden_width), jnp.bfloat16),
            *[pltpu.VMEM(chunk_shape, jnp.bfloat16) for _ in range(4)],
            pltpu.VMEM((rows, width), jnp.bfloat16),
            pltpu.VMEM((rows, width), jnp.bfloat16),
            pltpu.VMEM((rows, hidden_width), jnp.bfloat16),
            pltpu.VMEM((rows, hidden_width), jnp.float32),
            pltpu.VMEM((rows, hidden_width), jnp.bfloat16),
            pltpu.VMEM((8, width), jnp.float32),
            pltpu.VMEM((width, rows), jnp.bfloat16),
            pltpu.VMEM((rows, hidden_width), jnp.bfloat16),
            pltpu.VMEM((2, rows, width), jnp.bfloat16),
            pltpu.VMEM((2, width // 2, rows), jnp.bfloat16),
            pltpu.VMEM((2, width // 2, rows), jnp.bfloat16),
            pltpu.VMEM((2 * tiles, shards, block_rows, tile), jnp.bfloat16),
            pltpu.VMEM((2 * tiles, shards // 2, block_rows, tile), jnp.bfloat16),
            pltpu.VMEM((1, shards, block_rows, 128), jnp.bfloat16),
            *landing(2 * tiles, 0, tile),
            *landing(2 * tiles, 1, tile),
            *landing(1, 0, 128),
            dma((4,)),
            *[dma((chunks,)) for _ in range(4)],
            *[dma((2 * tiles, steps)) for _ in range(4)],
            *[dma((1, steps)) for _ in range(2)],
            *[dma((chunks, 2)) for _ in range(4)],
        ],
        compiler_params=pltpu.CompilerParams(
            collective_id=0, has_side_effects=True, vmem_limit_bytes=62 * 1024 * 1024
        ),
        cost_estimate=pl.CostEstimate(
            flops=2 * macs, bytes_accessed=8 * width * hidden_width, transcendentals=2 * rows * hidden_width
        ),
        name="window",
    )(
        drop_mask[0].reshape(micro * samples, layers),
        gain,
        x_in[0].reshape(chunk_shape),
        cotangent[0].reshape(chunk_shape),
        w_in[0],
        w_out[0],
    )
    return (grad_in[None], grad_out[None], grad_gain)


def solution(mesh):
    placed = (
        P("dp", None, None, None),
        P("dp", None, None, None),
        P("section", None, None),
        P("section", None, None),
        P("section", None),
        P("dp", None, None, None),
    )
    return jax.shard_map(
        per_device,
        mesh=mesh,
        in_specs=placed,
        out_specs=(P("section", "dp", None), P("section", "dp", None), P("section", "dp")),
        check_vma=False,
    )
```

```python
import functools

import jax
import jax.numpy as jnp
from jax import lax
from jax.experimental import pallas as pl
from jax.experimental.pallas import tpu as pltpu
from jax.sharding import PartitionSpec as P

EPSILON = 1e-05
ROOT_HALF = 0.7071067811865476
DENSITY_SCALE = 0.3989422804014327
MESH = pl.DeviceIdType.MESH

CHUNK_ROWS = 64
LAG = 3
HIDDEN_BLOCK = 512
TILE = 256
TRANSPOSED_RHS = (((1,), (1,)), ((), ()))


def largest_divisor(extent, limit, step):
    best = extent
    for size in range(step, min(extent, limit) + 1, step):
        if extent % size == 0:
            best = size
    return best


def position(block, order):
    place = 0
    for bit in order:
        place = 2 * place + ((block >> bit) & 1)
    return place


def kernel(
    dims, keep_ref, gain_ref, x_hbm, cot_hbm, w1_hbm, w2_hbm, grad_in_ref, grad_out_ref, grad_gain_ref,
    w1, w2, h_in, g_in, h_out, g_out, normed_all, gated_all, active_all, slope_all, hidden_grad_all,
    gain_sum, normed_t, active_far, gated_far, own_t, far_t, parts_a, parts_b, parts_g, *rest,
):
    sections, shards, chunk, chunks, seq_len, block, tile, tiles, steps = dims
    landed_a = rest[:steps]
    landed_b = rest[steps : 2 * steps - 1]
    landed_g = rest[2 * steps - 1 : 3 * steps - 1]
    (load_sem, h_send, h_recv, g_send, g_recv, a_send, a_recv, b_send, b_recv, e_send, e_recv,
     active_send, active_recv, gated_send, gated_recv) = rest[3 * steps - 1 :]
    width, hidden_width = w1.shape
    section = lax.axis_index("section")
    shard = lax.axis_index("dp")
    first, last = section == 0, section == sections - 1
    bits = [lax.rem(shard // (1 << b), 2) for b in range(steps)]
    partners = [shard + (1 - 2 * bits[b]) * (1 << b) for b in range(steps)]

    loads = [
        pltpu.make_async_copy(w1_hbm, w1, load_sem.at[0]),
        pltpu.make_async_copy(w2_hbm, w2, load_sem.at[1]),
    ]
    entry = pltpu.make_async_copy(x_hbm, h_in, load_sem.at[2])
    cotangents = pltpu.make_async_copy(cot_hbm, g_in, load_sem.at[3])
    pl.when(first)(entry.start)
    for load in loads:
        load.start()
    pl.when(last)(cotangents.start)

    barrier = pltpu.get_barrier_semaphore()

    def greet(where):
        pl.semaphore_signal(barrier, inc=1, device_id=where, device_id_type=MESH)

    pl.when(section > 0)(lambda: greet({"section": section - 1}))
    pl.when(section < sections - 1)(lambda: greet({"section": section + 1}))
    for partner in partners:
        greet({"dp": partner})
    neighbours = jnp.where(first, 0, 1) + jnp.where(last, 0, 1)
    pl.semaphore_wait(barrier, steps + neighbours)

    def h_copy(index):
        return pltpu.make_async_remote_copy(
            h_out.at[index], h_in.at[index], h_send.at[index], h_recv.at[index],
            device_id={"section": section + 1}, device_id_type=MESH,
        )

    def g_copy(index):
        return pltpu.make_async_remote_copy(
            g_out.at[index], g_in.at[index], g_send.at[index], g_recv.at[index],
            device_id={"section": section - 1}, device_id_type=MESH,
        )

    pair_bits = (1, steps - 1)
    half_width = hidden_width // 2

    def active_copy(index, half):
        rows = pl.ds(pl.multiple_of(index * chunk, chunk), chunk)
        columns = slice(half * half_width, (half + 1) * half_width)
        return pltpu.make_async_remote_copy(
            active_all.at[rows, columns], active_far.at[rows, columns],
            active_send.at[index, half], active_recv.at[index, half],
            device_id={"dp": partners[pair_bits[half]]}, device_id_type=MESH,
        )

    def gated_copy(index, half):
        rows = pl.ds(pl.multiple_of(index * chunk, chunk), chunk)
        return pltpu.make_async_remote_copy(
            gated_all.at[rows], gated_far.at[half, rows],
            gated_send.at[index, half], gated_recv.at[index, half],
            device_id={"dp": partners[pair_bits[half]]}, device_id_type=MESH,
        )

    gain_row = gain_ref[...].astype(jnp.float32)
    gain_sum[...] = jnp.zeros_like(gain_sum)
    column_blocks = [slice(at, at + block) for at in range(0, hidden_width, block)]

    orders_a = (list(range(steps)), [0] + list(range(steps - 1, 0, -1)))
    orders_b = tuple(
        [bit for bit in orders_a[1 - half] if bit != pair_bits[half]] for half in range(2)
    )
    block_rows = width // shards
    lots = 2 if chunks % 2 == 0 and chunks * chunk % 256 == 0 else 1
    lot_rows = chunks * chunk // lots

    def select_features(ref, half, turned, rows):
        bit, order = pair_bits[half], orders_b[half]

        def store(side):
            for place in range(shards // 2):
                at = sum(((place >> (len(order) - 1 - k)) & 1) << b for k, b in enumerate(order))
                at = (at + (side << bit)) * block_rows
                ref[half, place * block_rows : (place + 1) * block_rows, rows] = turned[
                    at : at + block_rows
                ].astype(jnp.bfloat16)

        for side in range(2):
            pl.when(bits[bit] == side)(lambda side=side: store(side))

    def turned_rows(rows_first):
        return (rows_first if block_rows % 16 == 0 else rows_first.astype(jnp.float32)).T

    def prepare(lot):
        def arrive(index, carry):
            for half in range(2):
                gated_copy(index, half).wait_recv()
            return carry

        lax.fori_loop(lot * (chunks // lots), (lot + 1) * (chunks // lots), arrive, 0)
        rows = slice(lot * lot_rows, (lot + 1) * lot_rows)
        turned = turned_rows(gated_all[rows, :])
        for half in range(2):
            select_features(own_t, half, turned, rows)
        for half in range(2):
            select_features(far_t, half, turned_rows(gated_far[half, rows]), rows)

    def prepare_early():
        for lot in range(lots - 1):
            prepare(lot)

    def keep_of(index):
        return keep_ref[(index * chunk) // seq_len, section].astype(jnp.float32)

    def forward(index):
        pl.when(section > 0)(lambda: h_copy(index).wait_recv())
        rows = pl.ds(pl.multiple_of(index * chunk, chunk), chunk)
        inputs = h_in[index].astype(jnp.float32)
        inv_rms = lax.rsqrt(jnp.mean(inputs * inputs, axis=-1, keepdims=True) + EPSILON)
        normed = (inputs * inv_rms * gain_row).astype(jnp.bfloat16)
        normed_all[rows, :] = normed
        branch = jnp.zeros((chunk, width), jnp.float32)
        for columns in column_blocks:
            hidden = jnp.dot(normed, w1[:, columns], preferred_element_type=jnp.float32)
            share = 0.5 * (1.0 + lax.erf(hidden * ROOT_HALF))
            active = (hidden * share).astype(jnp.bfloat16)
            active_all[rows, columns] = active
            slope_all[rows, columns] = share + hidden * jnp.exp(-0.5 * hidden * hidden) * DENSITY_SCALE
            branch += lax.dot_general(
                active, w2[:, columns], TRANSPOSED_RHS, preferred_element_type=jnp.float32
            )
        h_out[index] = (inputs + keep_of(index) * branch).astype(jnp.bfloat16)
        h_copy(index).start()
        for half in range(2):
            active_copy(index, half).start()

        @pl.when(index == chunks - 1)
        def _():
            normed_t[...] = normed_all[...].T

    def finish_chunk(index, inputs, inv_rms, upstream, grad_normed):
        @pl.when(section > 0)
        def _():
            scaled = grad_normed * gain_row
            centre = jnp.mean(scaled * inputs, axis=-1, keepdims=True)
            grads = upstream + inv_rms * (scaled - inputs * inv_rms * inv_rms * centre)
            g_out[index] = grads.astype(jnp.bfloat16)
            g_copy(index).start()

        gain_sum[0:1, :] += jnp.sum(grad_normed * inputs * inv_rms, axis=0, keepdims=True)

    def both(index):
        pl.when(index == chunks - 1)(prepare_early)
        pl.when(section > 0)(lambda: h_copy(index).wait_recv())
        rows = pl.ds(pl.multiple_of(index * chunk, chunk), chunk)
        inputs = h_in[index].astype(jnp.float32)
        inv_rms = lax.rsqrt(jnp.mean(inputs * inputs, axis=-1, keepdims=True) + EPSILON)
        normed = (inputs * inv_rms * gain_row).astype(jnp.bfloat16)
        normed_all[rows, :] = normed
        upstream = g_in[index].astype(jnp.float32)
        gated = gated_all[rows, :]
        grad_normed = jnp.zeros((chunk, width), jnp.float32)
        for columns in column_blocks:
            hidden = jnp.dot(normed, w1[:, columns], preferred_element_type=jnp.float32)
            grad_active = jnp.dot(gated, w2[:, columns], preferred_element_type=jnp.float32)
            share = 0.5 * (1.0 + lax.erf(hidden * ROOT_HALF))
            active_all[rows, columns] = (hidden * share).astype(jnp.bfloat16)
            slope = share + hidden * jnp.exp(-0.5 * hidden * hidden) * DENSITY_SCALE
            grad_hidden = (grad_active * slope).astype(jnp.bfloat16)
            hidden_grad_all[rows, columns] = grad_hidden
            grad_normed += lax.dot_general(
                grad_hidden, w1[:, columns], TRANSPOSED_RHS, preferred_element_type=jnp.float32
            )
        for half in range(2):
            active_copy(index, half).start()
        finish_chunk(index, inputs, inv_rms, upstream, grad_normed)

        @pl.when(index == chunks - 1)
        def _():
            normed_t[...] = normed_all[...].T

    def backward(index):
        pl.when(index == chunks - 1)(prepare_early)
        g_copy(index).wait_recv()
        rows = pl.ds(pl.multiple_of(index * chunk, chunk), chunk)
        inputs = h_in[index].astype(jnp.float32)
        inv_rms = lax.rsqrt(jnp.mean(inputs * inputs, axis=-1, keepdims=True) + EPSILON)
        upstream = g_in[index].astype(jnp.float32)
        gated = (keep_of(index) * upstream).astype(jnp.bfloat16)
        gated_all[rows, :] = gated
        for half in range(2):
            gated_copy(index, half).start()
        grad_normed = jnp.zeros((chunk, width), jnp.float32)
        for columns in column_blocks:
            grad_active = jnp.dot(gated, w2[:, columns], preferred_element_type=jnp.float32)
            grad_hidden = (grad_active * slope_all[rows, columns]).astype(jnp.bfloat16)
            hidden_grad_all[rows, columns] = grad_hidden
            grad_normed += lax.dot_general(
                grad_hidden, w1[:, columns], TRANSPOSED_RHS, preferred_element_type=jnp.float32
            )
        finish_chunk(index, inputs, inv_rms, upstream, grad_normed)

    pl.when(first)(entry.wait)
    for load in loads:
        load.wait()
    pl.when(last)(cotangents.wait)

    def tick(moment, carry):
        ahead = moment - LAG * section
        behind = moment - LAG * (2 * (sections - 1) - section)
        pl.when(jnp.logical_and(ahead >= 0, ahead < chunks))(lambda: forward(ahead))
        pl.when(jnp.logical_and(behind >= 0, behind < chunks))(lambda: backward(behind))
        return carry

    def send_gated(index, carry):
        rows = pl.ds(pl.multiple_of(index * chunk, chunk), chunk)
        gated_all[rows, :] = (keep_of(index) * g_in[index].astype(jnp.float32)).astype(jnp.bfloat16)
        for half in range(2):
            gated_copy(index, half).start()
        return carry

    def last_tick(index, carry):
        both(index)
        return carry

    @pl.when(last)
    def _():
        lax.fori_loop(0, chunks, send_gated, 0)
        lax.fori_loop(0, chunks, last_tick, 0)

    @pl.when(section < sections - 1)
    def _():
        lax.fori_loop(0, chunks + 2 * LAG * (sections - 1), tick, 0)

    def halving(order, parts, landed, send_sem, recv_sem):
        count = 1 << len(order)

        def copy(at, step):
            half = count >> (step + 1)
            bit = order[step]
            source = parts if step == 0 else landed[step - 1]
            return pltpu.make_async_remote_copy(
                source.at[at, pl.ds((1 - bits[bit]) * half, half)],
                landed[step].at[at],
                send_sem.at[at, step],
                recv_sem.at[at, step],
                device_id={"dp": partners[bit]},
                device_id_type=MESH,
            )

        def fill(at, value, places):
            for number, place in enumerate(places):
                rows = value[number * block_rows : (number + 1) * block_rows]
                parts[at, place] = rows.astype(jnp.bfloat16)
            copy(at, 0).start()

        def advance(at, step, finish):
            copy(at, step).wait_recv()
            half = count >> (step + 1)
            source = parts if step == 0 else landed[step - 1]
            own = source[at, pl.ds(bits[order[step]] * half, half)].astype(jnp.float32)
            total = own + landed[step][at].astype(jnp.float32)
            if step + 1 < len(order):
                landed[step][at] = total.astype(jnp.bfloat16)
                copy(at, step + 1).start()
            else:
                finish(total[0])

        def close(at):
            for step in range(len(order)):
                copy(at, step).wait_send()

        return fill, advance, close

    streams_a = [halving(order, parts_a, landed_a, a_send, a_recv) for order in orders_a]
    streams_b = [halving(order, parts_b, landed_b, b_send, b_recv) for order in orders_b]
    fill_g, advance_g, close_g = halving(orders_a[0], parts_g, landed_g, e_send, e_recv)

    def finish_gain(total):
        grad_gain_ref[...] = jnp.transpose(total)[0:1, :]

    def columns_of(at, half):
        return pl.ds(pl.multiple_of(at * tile + half * half_width, tile), tile)

    def active_arrives(index, carry):
        for half in range(2):
            active_copy(index, half).wait_recv()
        return carry

    def finish(out_ref, at, half):
        def store(total):
            out_ref[:, columns_of(at, half)] = total

        return store

    def within(at):
        return pl.when(jnp.logical_and(at >= 0, at < tiles))

    def advance_all(streams, out_ref, at, step):
        @within(at)
        def _():
            for half in range(2):
                streams[half][1](half * tiles + at, step, finish(out_ref, at, half))

    def turn(moment, carry):
        advance_all(streams_a, grad_in_ref, moment - 1, 0)
        advance_all(streams_b, grad_out_ref, moment - 2, 0)

        @within(moment)
        def _():
            for half in range(2):
                value = jnp.dot(
                    normed_t[...],
                    hidden_grad_all[:, columns_of(moment, half)],
                    preferred_element_type=jnp.float32,
                )
                places = [position(b, orders_a[half]) for b in range(shards)]
                streams_a[half][0](half * tiles + moment, value, places)

        @pl.when(moment == 1)
        def _():
            prepare(lots - 1)
            lax.fori_loop(0, chunks, active_arrives, 0)
            gain_lanes = jnp.broadcast_to(gain_sum[0:1, :], (128, width)).T
            fill_g(0, gain_lanes, [position(b, orders_a[0]) for b in range(shards)])

        @within(moment - 1)
        def _():
            for half in range(2):
                columns = columns_of(moment - 1, half)
                value = jnp.dot(
                    own_t[half], active_all[:, columns], preferred_element_type=jnp.float32
                ) + jnp.dot(far_t[half], active_far[:, columns], preferred_element_type=jnp.float32)
                streams_b[half][0](half * tiles + moment - 1, value, range(shards // 2))

        for step in range(1, steps):
            advance_all(streams_a, grad_in_ref, moment - (step + 1), step)
            if step + 1 < steps:
                advance_all(streams_b, grad_out_ref, moment - (step + 2), step)
        for step in range(steps):
            pl.when(moment == step + 2)(lambda step=step: advance_g(0, step, finish_gain))
        return carry

    lax.fori_loop(0, max(tiles, 2) + steps, turn, 0)

    def close_chunk(index, carry):
        pl.when(section < sections - 1)(lambda: h_copy(index).wait_send())
        pl.when(section > 0)(lambda: g_copy(index).wait_send())
        for half in range(2):
            active_copy(index, half).wait_send()
            gated_copy(index, half).wait_send()
        return carry

    lax.fori_loop(0, chunks, close_chunk, 0)

    def close_tile(at, carry):
        for half in range(2):
            streams_a[half][2](half * tiles + at)
            streams_b[half][2](half * tiles + at)
        return carry

    lax.fori_loop(0, tiles, close_tile, 0)
    close_g(0)


def per_device(x_in, cotangent, w_in, w_out, gain, drop_mask):
    sections = lax.axis_size("section")
    shards = lax.axis_size("dp")
    micro, micro_rows, width = x_in.shape[1:]
    hidden_width = w_in.shape[2]
    samples, layers = drop_mask.shape[2:]
    seq_len = micro_rows // samples
    rows = micro * micro_rows
    chunk = largest_divisor(seq_len, CHUNK_ROWS, 16)
    chunks = rows // chunk
    block = largest_divisor(hidden_width, HIDDEN_BLOCK, 128)
    tile = largest_divisor(hidden_width // 2, TILE, 128)
    tiles = hidden_width // 2 // tile
    steps = shards.bit_length() - 1
    assert shards == 1 << steps and steps >= 2
    block_rows = width // shards
    dims = (sections, shards, chunk, chunks, seq_len, block, tile, tiles, steps)

    def landing(count, start, columns):
        return [
            pltpu.VMEM((count, shards >> (step + 1), block_rows, columns), jnp.bfloat16)
            for step in range(start, steps)
        ]

    chunk_shape = (chunks, chunk, width)
    any_spec = pl.BlockSpec(memory_space=pl.ANY)
    vmem_spec = pl.BlockSpec(memory_space=pltpu.VMEM)
    dma = pltpu.SemaphoreType.DMA
    macs = 6 * rows * width * hidden_width
    grad_in, grad_out, grad_gain = pl.pallas_call(
        functools.partial(kernel, dims),
        out_shape=(
            jax.ShapeDtypeStruct((block_rows, hidden_width), jnp.float32),
            jax.ShapeDtypeStruct((block_rows, hidden_width), jnp.float32),
            jax.ShapeDtypeStruct((1, block_rows), jnp.float32),
        ),
        in_specs=[pl.BlockSpec(memory_space=pltpu.SMEM), vmem_spec] + [any_spec] * 4,
        out_specs=(vmem_spec,) * 3,
        scratch_shapes=[
            pltpu.VMEM((width, hidden_width), jnp.bfloat16),
            pltpu.VMEM((width, hidden_width), jnp.bfloat16),
            *[pltpu.VMEM(chunk_shape, jnp.bfloat16) for _ in range(4)],
            pltpu.VMEM((rows, width), jnp.bfloat16),
            pltpu.VMEM((rows, width), jnp.bfloat16),
            pltpu.VMEM((rows, hidden_width), jnp.bfloat16),
            pltpu.VMEM((rows, hidden_width), jnp.float32),
            pltpu.VMEM((rows, hidden_width), jnp.bfloat16),
            pltpu.VMEM((8, width), jnp.float32),
            pltpu.VMEM((width, rows), jnp.bfloat16),
            pltpu.VMEM((rows, hidden_width), jnp.bfloat16),
            pltpu.VMEM((2, rows, width), jnp.bfloat16),
            pltpu.VMEM((2, width // 2, rows), jnp.bfloat16),
            pltpu.VMEM((2, width // 2, rows), jnp.bfloat16),
            pltpu.VMEM((2 * tiles, shards, block_rows, tile), jnp.bfloat16),
            pltpu.VMEM((2 * tiles, shards // 2, block_rows, tile), jnp.bfloat16),
            pltpu.VMEM((1, shards, block_rows, 128), jnp.bfloat16),
            *landing(2 * tiles, 0, tile),
            *landing(2 * tiles, 1, tile),
            *landing(1, 0, 128),
            dma((4,)),
            *[dma((chunks,)) for _ in range(4)],
            *[dma((2 * tiles, steps)) for _ in range(4)],
            *[dma((1, steps)) for _ in range(2)],
            *[dma((chunks, 2)) for _ in range(4)],
        ],
        compiler_params=pltpu.CompilerParams(
            collective_id=0, has_side_effects=True, vmem_limit_bytes=62 * 1024 * 1024
        ),
        cost_estimate=pl.CostEstimate(
            flops=2 * macs, bytes_accessed=8 * width * hidden_width, transcendentals=2 * rows * hidden_width
        ),
        name="window",
    )(
        drop_mask[0].reshape(micro * samples, layers),
        gain,
        x_in[0].reshape(chunk_shape),
        cotangent[0].reshape(chunk_shape),
        w_in[0],
        w_out[0],
    )
    return (grad_in[None], grad_out[None], grad_gain)


def solution(mesh):
    placed = (
        P("dp", None, None, None),
        P("dp", None, None, None),
        P("section", None, None),
        P("section", None, None),
        P("section", None),
        P("dp", None, None, None),
    )
    return jax.shard_map(
        per_device,
        mesh=mesh,
        in_specs=placed,
        out_specs=(P("section", "dp", None), P("section", "dp", None), P("section", "dp")),
        check_vma=False,
    )
```

```python
import functools

import jax
import jax.numpy as jnp
from jax import lax
from jax.experimental import pallas as pl
from jax.experimental.pallas import tpu as pltpu
from jax.sharding import PartitionSpec as P

EPSILON = 1e-05
ROOT_HALF = 0.7071067811865476
DENSITY_SCALE = 0.3989422804014327
MESH = pl.DeviceIdType.MESH

CHUNK_ROWS = 64
LAG = 3
HIDDEN_BLOCK = 512
TILE = 256
TRANSPOSED_RHS = (((1,), (1,)), ((), ()))


def largest_divisor(extent, limit, step):
    best = extent
    for size in range(step, min(extent, limit) + 1, step):
        if extent % size == 0:
            best = size
    return best


def position(block, order):
    place = 0
    for bit in order:
        place = 2 * place + ((block >> bit) & 1)
    return place


def kernel(
    dims, keep_ref, gain_ref, x_hbm, cot_hbm, w1_hbm, w2_hbm, grad_in_ref, grad_out_ref, grad_gain_ref,
    w1, w2, h_in, g_in, h_out, g_out, normed_all, gated_all, active_all, slope_all, hidden_grad_all,
    gain_sum, normed_t, active_far, gated_far, own_t, far_t, parts_a, parts_b, parts_g, *rest,
):
    sections, shards, chunk, chunks, seq_len, block, tile, tiles, steps = dims
    landed_a = rest[:steps]
    landed_b = rest[steps : 2 * steps - 1]
    landed_g = rest[2 * steps - 1 : 3 * steps - 1]
    (load_sem, h_send, h_recv, g_send, g_recv, a_send, a_recv, b_send, b_recv, e_send, e_recv,
     active_send, active_recv, gated_send, gated_recv) = rest[3 * steps - 1 :]
    width, hidden_width = w1.shape
    section = lax.axis_index("section")
    shard = lax.axis_index("dp")
    first, last = section == 0, section == sections - 1
    bits = [lax.rem(shard // (1 << b), 2) for b in range(steps)]
    partners = [shard + (1 - 2 * bits[b]) * (1 << b) for b in range(steps)]

    loads = [
        pltpu.make_async_copy(w1_hbm, w1, load_sem.at[0]),
        pltpu.make_async_copy(w2_hbm, w2, load_sem.at[1]),
    ]
    entry = pltpu.make_async_copy(x_hbm, h_in, load_sem.at[2])
    cotangents = pltpu.make_async_copy(cot_hbm, g_in, load_sem.at[3])
    pl.when(first)(entry.start)
    for load in loads:
        load.start()
    pl.when(last)(cotangents.start)

    barrier = pltpu.get_barrier_semaphore()

    def greet(where):
        pl.semaphore_signal(barrier, inc=1, device_id=where, device_id_type=MESH)

    pl.when(section > 0)(lambda: greet({"section": section - 1}))
    pl.when(section < sections - 1)(lambda: greet({"section": section + 1}))
    for partner in partners:
        greet({"dp": partner})
    neighbours = jnp.where(first, 0, 1) + jnp.where(last, 0, 1)
    pl.semaphore_wait(barrier, steps + neighbours)

    def h_copy(index):
        return pltpu.make_async_remote_copy(
            h_out.at[index], h_in.at[index], h_send.at[index], h_recv.at[index],
            device_id={"section": section + 1}, device_id_type=MESH,
        )

    def g_copy(index):
        return pltpu.make_async_remote_copy(
            g_out.at[index], g_in.at[index], g_send.at[index], g_recv.at[index],
            device_id={"section": section - 1}, device_id_type=MESH,
        )

    pair_bits = (1, steps - 1)
    half_width = hidden_width // 2

    def active_copy(index, half):
        rows = pl.ds(pl.multiple_of(index * chunk, chunk), chunk)
        columns = slice(half * half_width, (half + 1) * half_width)
        return pltpu.make_async_remote_copy(
            active_all.at[rows, columns], active_far.at[rows, columns],
            active_send.at[index, half], active_recv.at[index, half],
            device_id={"dp": partners[pair_bits[half]]}, device_id_type=MESH,
        )

    def gated_copy(index, half):
        rows = pl.ds(pl.multiple_of(index * chunk, chunk), chunk)
        return pltpu.make_async_remote_copy(
            gated_all.at[rows], gated_far.at[half, rows],
            gated_send.at[index, half], gated_recv.at[index, half],
            device_id={"dp": partners[pair_bits[half]]}, device_id_type=MESH,
        )

    gain_row = gain_ref[...].astype(jnp.float32)
    gain_sum[...] = jnp.zeros_like(gain_sum)
    column_blocks = [slice(at, at + block) for at in range(0, hidden_width, block)]

    orders_a = (list(range(steps)), [0] + list(range(steps - 1, 0, -1)))
    orders_b = tuple(
        [bit for bit in orders_a[1 - half] if bit != pair_bits[half]] for half in range(2)
    )
    block_rows = width // shards
    lots = 2 if chunks % 2 == 0 and chunks * chunk % 256 == 0 else 1
    lot_rows = chunks * chunk // lots

    def select_features(ref, half, turned, rows):
        bit, order = pair_bits[half], orders_b[half]

        def store(side):
            for place in range(shards // 2):
                at = sum(((place >> (len(order) - 1 - k)) & 1) << b for k, b in enumerate(order))
                at = (at + (side << bit)) * block_rows
                ref[half, place * block_rows : (place + 1) * block_rows, rows] = turned[
                    at : at + block_rows
                ].astype(jnp.bfloat16)

        for side in range(2):
            pl.when(bits[bit] == side)(lambda side=side: store(side))

    def turned_rows(rows_first):
        return (rows_first if block_rows % 16 == 0 else rows_first.astype(jnp.float32)).T

    def prepare(lot):
        def arrive(index, carry):
            for half in range(2):
                gated_copy(index, half).wait_recv()
            return carry

        lax.fori_loop(lot * (chunks // lots), (lot + 1) * (chunks // lots), arrive, 0)
        rows = slice(lot * lot_rows, (lot + 1) * lot_rows)
        turned = turned_rows(gated_all[rows, :])
        for half in range(2):
            select_features(own_t, half, turned, rows)
        for half in range(2):
            select_features(far_t, half, turned_rows(gated_far[half, rows]), rows)

    def prepare_early():
        for lot in range(lots - 1):
            prepare(lot)

    def keep_of(index):
        return keep_ref[(index * chunk) // seq_len, section].astype(jnp.float32)

    def forward(index):
        pl.when(section > 0)(lambda: h_copy(index).wait_recv())
        rows = pl.ds(pl.multiple_of(index * chunk, chunk), chunk)
        inputs = h_in[index].astype(jnp.float32)
        inv_rms = lax.rsqrt(jnp.mean(inputs * inputs, axis=-1, keepdims=True) + EPSILON)
        normed = (inputs * inv_rms * gain_row).astype(jnp.bfloat16)
        normed_all[rows, :] = normed
        branch = jnp.zeros((chunk, width), jnp.float32)
        for columns in column_blocks:
            hidden = jnp.dot(normed, w1[:, columns], preferred_element_type=jnp.float32)
            share = 0.5 * (1.0 + lax.erf(hidden * ROOT_HALF))
            active = (hidden * share).astype(jnp.bfloat16)
            active_all[rows, columns] = active
            slope_all[rows, columns] = share + hidden * jnp.exp(-0.5 * hidden * hidden) * DENSITY_SCALE
            branch += lax.dot_general(
                active, w2[:, columns], TRANSPOSED_RHS, preferred_element_type=jnp.float32
            )
        h_out[index] = (inputs + keep_of(index) * branch).astype(jnp.bfloat16)
        h_copy(index).start()
        for half in range(2):
            active_copy(index, half).start()

        @pl.when(index == chunks - 1)
        def _():
            normed_t[...] = normed_all[...].T

    def finish_chunk(index, inputs, inv_rms, upstream, grad_normed):
        @pl.when(section > 0)
        def _():
            scaled = grad_normed * gain_row
            centre = jnp.mean(scaled * inputs, axis=-1, keepdims=True)
            grads = upstream + inv_rms * (scaled - inputs * inv_rms * inv_rms * centre)
            g_out[index] = grads.astype(jnp.bfloat16)
            g_copy(index).start()

        gain_sum[0:1, :] += jnp.sum(grad_normed * inputs * inv_rms, axis=0, keepdims=True)

    def both(index):
        pl.when(section > 0)(lambda: h_copy(index).wait_recv())
        rows = pl.ds(pl.multiple_of(index * chunk, chunk), chunk)
        inputs = h_in[index].astype(jnp.float32)
        inv_rms = lax.rsqrt(jnp.mean(inputs * inputs, axis=-1, keepdims=True) + EPSILON)
        normed = (inputs * inv_rms * gain_row).astype(jnp.bfloat16)
        normed_all[rows, :] = normed
        upstream = g_in[index].astype(jnp.float32)
        gated = gated_all[rows, :]
        grad_normed = jnp.zeros((chunk, width), jnp.float32)
        for columns in column_blocks:
            hidden = jnp.dot(normed, w1[:, columns], preferred_element_type=jnp.float32)
            grad_active = jnp.dot(gated, w2[:, columns], preferred_element_type=jnp.float32)
            share = 0.5 * (1.0 + lax.erf(hidden * ROOT_HALF))
            active_all[rows, columns] = (hidden * share).astype(jnp.bfloat16)
            slope = share + hidden * jnp.exp(-0.5 * hidden * hidden) * DENSITY_SCALE
            grad_hidden = (grad_active * slope).astype(jnp.bfloat16)
            hidden_grad_all[rows, columns] = grad_hidden
            grad_normed += lax.dot_general(
                grad_hidden, w1[:, columns], TRANSPOSED_RHS, preferred_element_type=jnp.float32
            )
        for half in range(2):
            active_copy(index, half).start()
        finish_chunk(index, inputs, inv_rms, upstream, grad_normed)

        @pl.when(index == chunks - 1)
        def _():
            normed_t[...] = normed_all[...].T

    def backward(index):
        pl.when(index == chunks // 2 + 1)(prepare_early)
        g_copy(index).wait_recv()
        rows = pl.ds(pl.multiple_of(index * chunk, chunk), chunk)
        inputs = h_in[index].astype(jnp.float32)
        inv_rms = lax.rsqrt(jnp.mean(inputs * inputs, axis=-1, keepdims=True) + EPSILON)
        upstream = g_in[index].astype(jnp.float32)
        gated = (keep_of(index) * upstream).astype(jnp.bfloat16)
        gated_all[rows, :] = gated
        for half in range(2):
            gated_copy(index, half).start()
        grad_normed = jnp.zeros((chunk, width), jnp.float32)
        for columns in column_blocks:
            grad_active = jnp.dot(gated, w2[:, columns], preferred_element_type=jnp.float32)
            grad_hidden = (grad_active * slope_all[rows, columns]).astype(jnp.bfloat16)
            hidden_grad_all[rows, columns] = grad_hidden
            grad_normed += lax.dot_general(
                grad_hidden, w1[:, columns], TRANSPOSED_RHS, preferred_element_type=jnp.float32
            )
        finish_chunk(index, inputs, inv_rms, upstream, grad_normed)

    pl.when(first)(entry.wait)
    for load in loads:
        load.wait()
    pl.when(last)(cotangents.wait)

    def tick(moment, carry):
        ahead = moment - LAG * section
        behind = moment - LAG * (2 * (sections - 1) - section)
        pl.when(jnp.logical_and(ahead >= 0, ahead < chunks))(lambda: forward(ahead))
        pl.when(jnp.logical_and(behind >= 0, behind < chunks))(lambda: backward(behind))
        return carry

    def send_gated(index, carry):
        rows = pl.ds(pl.multiple_of(index * chunk, chunk), chunk)
        gated_all[rows, :] = (keep_of(index) * g_in[index].astype(jnp.float32)).astype(jnp.bfloat16)
        for half in range(2):
            gated_copy(index, half).start()
        return carry

    def last_tick(index, carry):
        both(index)
        return carry

    @pl.when(last)
    def _():
        lax.fori_loop(0, chunks, send_gated, 0)
        for lot in range(lots):
            prepare(lot)
        lax.fori_loop(0, chunks, last_tick, 0)

    @pl.when(section < sections - 1)
    def _():
        lax.fori_loop(0, chunks + 2 * LAG * (sections - 1), tick, 0)

    def halving(order, parts, landed, send_sem, recv_sem):
        count = 1 << len(order)

        def copy(at, step):
            half = count >> (step + 1)
            bit = order[step]
            source = parts if step == 0 else landed[step - 1]
            return pltpu.make_async_remote_copy(
                source.at[at, pl.ds((1 - bits[bit]) * half, half)],
                landed[step].at[at],
                send_sem.at[at, step],
                recv_sem.at[at, step],
                device_id={"dp": partners[bit]},
                device_id_type=MESH,
            )

        def fill(at, value, places):
            for number, place in enumerate(places):
                rows = value[number * block_rows : (number + 1) * block_rows]
                parts[at, place] = rows.astype(jnp.bfloat16)
            copy(at, 0).start()

        def advance(at, step, finish):
            copy(at, step).wait_recv()
            half = count >> (step + 1)
            source = parts if step == 0 else landed[step - 1]
            own = source[at, pl.ds(bits[order[step]] * half, half)].astype(jnp.float32)
            total = own + landed[step][at].astype(jnp.float32)
            if step + 1 < len(order):
                landed[step][at] = total.astype(jnp.bfloat16)
                copy(at, step + 1).start()
            else:
                finish(total[0])

        def close(at):
            for step in range(len(order)):
                copy(at, step).wait_send()

        return fill, advance, close

    streams_a = [halving(order, parts_a, landed_a, a_send, a_recv) for order in orders_a]
    streams_b = [halving(order, parts_b, landed_b, b_send, b_recv) for order in orders_b]
    fill_g, advance_g, close_g = halving(orders_a[0], parts_g, landed_g, e_send, e_recv)

    def finish_gain(total):
        grad_gain_ref[...] = jnp.transpose(total)[0:1, :]

    def columns_of(at, half):
        return pl.ds(pl.multiple_of(at * tile + half * half_width, tile), tile)

    def active_arrives(index, carry):
        for half in range(2):
            active_copy(index, half).wait_recv()
        return carry

    def finish(out_ref, at, half):
        def store(total):
            out_ref[:, columns_of(at, half)] = total

        return store

    def within(at):
        return pl.when(jnp.logical_and(at >= 0, at < tiles))

    def advance_all(streams, out_ref, at, step):
        @within(at)
        def _():
            for half in range(2):
                streams[half][1](half * tiles + at, step, finish(out_ref, at, half))

    def turn(moment, carry):
        advance_all(streams_a, grad_in_ref, moment - 1, 0)
        advance_all(streams_b, grad_out_ref, moment - 2, 0)

        @within(moment)
        def _():
            for half in range(2):
                value = jnp.dot(
                    normed_t[...],
                    hidden_grad_all[:, columns_of(moment, half)],
                    preferred_element_type=jnp.float32,
                )
                places = [position(b, orders_a[half]) for b in range(shards)]
                streams_a[half][0](half * tiles + moment, value, places)

        @pl.when(moment == 1)
        def _():
            pl.when(section < sections - 1)(lambda: prepare(lots - 1))
            lax.fori_loop(0, chunks, active_arrives, 0)
            gain_lanes = jnp.broadcast_to(gain_sum[0:1, :], (128, width)).T
            fill_g(0, gain_lanes, [position(b, orders_a[0]) for b in range(shards)])

        @within(moment - 1)
        def _():
            for half in range(2):
                columns = columns_of(moment - 1, half)
                value = jnp.dot(
                    own_t[half], active_all[:, columns], preferred_element_type=jnp.float32
                ) + jnp.dot(far_t[half], active_far[:, columns], preferred_element_type=jnp.float32)
                streams_b[half][0](half * tiles + moment - 1, value, range(shards // 2))

        for step in range(1, steps):
            advance_all(streams_a, grad_in_ref, moment - (step + 1), step)
            if step + 1 < steps:
                advance_all(streams_b, grad_out_ref, moment - (step + 2), step)
        for step in range(steps):
            pl.when(moment == step + 2)(lambda step=step: advance_g(0, step, finish_gain))
        return carry

    lax.fori_loop(0, max(tiles, 2) + steps, turn, 0)

    def close_chunk(index, carry):
        pl.when(section < sections - 1)(lambda: h_copy(index).wait_send())
        pl.when(section > 0)(lambda: g_copy(index).wait_send())
        for half in range(2):
            active_copy(index, half).wait_send()
            gated_copy(index, half).wait_send()
        return carry

    lax.fori_loop(0, chunks, close_chunk, 0)

    def close_tile(at, carry):
        for half in range(2):
            streams_a[half][2](half * tiles + at)
            streams_b[half][2](half * tiles + at)
        return carry

    lax.fori_loop(0, tiles, close_tile, 0)
    close_g(0)


def per_device(x_in, cotangent, w_in, w_out, gain, drop_mask):
    sections = lax.axis_size("section")
    shards = lax.axis_size("dp")
    micro, micro_rows, width = x_in.shape[1:]
    hidden_width = w_in.shape[2]
    samples, layers = drop_mask.shape[2:]
    seq_len = micro_rows // samples
    rows = micro * micro_rows
    chunk = largest_divisor(seq_len, CHUNK_ROWS, 16)
    chunks = rows // chunk
    block = largest_divisor(hidden_width, HIDDEN_BLOCK, 128)
    tile = largest_divisor(hidden_width // 2, TILE, 128)
    tiles = hidden_width // 2 // tile
    steps = shards.bit_length() - 1
    assert shards == 1 << steps and steps >= 2
    block_rows = width // shards
    dims = (sections, shards, chunk, chunks, seq_len, block, tile, tiles, steps)

    def landing(count, start, columns):
        return [
            pltpu.VMEM((count, shards >> (step + 1), block_rows, columns), jnp.bfloat16)
            for step in range(start, steps)
        ]

    chunk_shape = (chunks, chunk, width)
    any_spec = pl.BlockSpec(memory_space=pl.ANY)
    vmem_spec = pl.BlockSpec(memory_space=pltpu.VMEM)
    dma = pltpu.SemaphoreType.DMA
    macs = 6 * rows * width * hidden_width
    grad_in, grad_out, grad_gain = pl.pallas_call(
        functools.partial(kernel, dims),
        out_shape=(
            jax.ShapeDtypeStruct((block_rows, hidden_width), jnp.float32),
            jax.ShapeDtypeStruct((block_rows, hidden_width), jnp.float32),
            jax.ShapeDtypeStruct((1, block_rows), jnp.float32),
        ),
        in_specs=[pl.BlockSpec(memory_space=pltpu.SMEM), vmem_spec] + [any_spec] * 4,
        out_specs=(vmem_spec,) * 3,
        scratch_shapes=[
            pltpu.VMEM((width, hidden_width), jnp.bfloat16),
            pltpu.VMEM((width, hidden_width), jnp.bfloat16),
            *[pltpu.VMEM(chunk_shape, jnp.bfloat16) for _ in range(4)],
            pltpu.VMEM((rows, width), jnp.bfloat16),
            pltpu.VMEM((rows, width), jnp.bfloat16),
            pltpu.VMEM((rows, hidden_width), jnp.bfloat16),
            pltpu.VMEM((rows, hidden_width), jnp.float32),
            pltpu.VMEM((rows, hidden_width), jnp.bfloat16),
            pltpu.VMEM((8, width), jnp.float32),
            pltpu.VMEM((width, rows), jnp.bfloat16),
            pltpu.VMEM((rows, hidden_width), jnp.bfloat16),
            pltpu.VMEM((2, rows, width), jnp.bfloat16),
            pltpu.VMEM((2, width // 2, rows), jnp.bfloat16),
            pltpu.VMEM((2, width // 2, rows), jnp.bfloat16),
            pltpu.VMEM((2 * tiles, shards, block_rows, tile), jnp.bfloat16),
            pltpu.VMEM((2 * tiles, shards // 2, block_rows, tile), jnp.bfloat16),
            pltpu.VMEM((1, shards, block_rows, 128), jnp.bfloat16),
            *landing(2 * tiles, 0, tile),
            *landing(2 * tiles, 1, tile),
            *landing(1, 0, 128),
            dma((4,)),
            *[dma((chunks,)) for _ in range(4)],
            *[dma((2 * tiles, steps)) for _ in range(4)],
            *[dma((1, steps)) for _ in range(2)],
            *[dma((chunks, 2)) for _ in range(4)],
        ],
        compiler_params=pltpu.CompilerParams(
            collective_id=0, has_side_effects=True, vmem_limit_bytes=62 * 1024 * 1024
        ),
        cost_estimate=pl.CostEstimate(
            flops=2 * macs, bytes_accessed=8 * width * hidden_width, transcendentals=2 * rows * hidden_width
        ),
        name="window",
    )(
        drop_mask[0].reshape(micro * samples, layers),
        gain,
        x_in[0].reshape(chunk_shape),
        cotangent[0].reshape(chunk_shape),
        w_in[0],
        w_out[0],
    )
    return (grad_in[None], grad_out[None], grad_gain)


def solution(mesh):
    placed = (
        P("dp", None, None, None),
        P("dp", None, None, None),
        P("section", None, None),
        P("section", None, None),
        P("section", None),
        P("dp", None, None, None),
    )
    return jax.shard_map(
        per_device,
        mesh=mesh,
        in_specs=placed,
        out_specs=(P("section", "dp", None), P("section", "dp", None), P("section", "dp")),
        check_vma=False,
    )
```

```python
import functools

import jax
import jax.numpy as jnp
from jax import lax
from jax.experimental import pallas as pl
from jax.experimental.pallas import tpu as pltpu
from jax.sharding import PartitionSpec as P

EPSILON = 1e-05
ROOT_HALF = 0.7071067811865476
DENSITY_SCALE = 0.3989422804014327
MESH = pl.DeviceIdType.MESH

CHUNK_ROWS = 64
LAG = 3
HIDDEN_BLOCK = 512
TILE = 256
TRANSPOSED_RHS = (((1,), (1,)), ((), ()))


def largest_divisor(extent, limit, step):
    best = extent
    for size in range(step, min(extent, limit) + 1, step):
        if extent % size == 0:
            best = size
    return best


def position(block, order):
    place = 0
    for bit in order:
        place = 2 * place + ((block >> bit) & 1)
    return place


def kernel(
    dims, keep_ref, gain_ref, x_hbm, cot_hbm, w1_hbm, w2_hbm, grad_in_ref, grad_out_ref, grad_gain_ref,
    w1, w2, h_in, g_in, h_out, g_out, normed_all, gated_all, active_all, slope_all, hidden_grad_all,
    gain_sum, normed_t, active_far, gated_far, own_t, far_t, parts_a, parts_b, parts_g, *rest,
):
    sections, shards, chunk, chunks, seq_len, block, tile, tiles, steps = dims
    landed_a = rest[:steps]
    landed_b = rest[steps : 2 * steps - 1]
    landed_g = rest[2 * steps - 1 : 3 * steps - 1]
    (load_sem, h_send, h_recv, g_send, g_recv, a_send, a_recv, b_send, b_recv, e_send, e_recv,
     active_send, active_recv, gated_send, gated_recv) = rest[3 * steps - 1 :]
    width, hidden_width = w1.shape
    section = lax.axis_index("section")
    shard = lax.axis_index("dp")
    first, last = section == 0, section == sections - 1
    bits = [lax.rem(shard // (1 << b), 2) for b in range(steps)]
    partners = [shard + (1 - 2 * bits[b]) * (1 << b) for b in range(steps)]

    loads = [
        pltpu.make_async_copy(w1_hbm, w1, load_sem.at[0]),
        pltpu.make_async_copy(w2_hbm, w2, load_sem.at[1]),
    ]
    entry = pltpu.make_async_copy(x_hbm, h_in, load_sem.at[2])
    cotangents = pltpu.make_async_copy(cot_hbm, g_in, load_sem.at[3])
    pl.when(first)(entry.start)
    for load in loads:
        load.start()
    pl.when(last)(cotangents.start)

    barrier = pltpu.get_barrier_semaphore()

    def greet(where):
        pl.semaphore_signal(barrier, inc=1, device_id=where, device_id_type=MESH)

    pl.when(section > 0)(lambda: greet({"section": section - 1}))
    pl.when(section < sections - 1)(lambda: greet({"section": section + 1}))
    for partner in partners:
        greet({"dp": partner})
    neighbours = jnp.where(first, 0, 1) + jnp.where(last, 0, 1)
    pl.semaphore_wait(barrier, steps + neighbours)

    def h_copy(index):
        return pltpu.make_async_remote_copy(
            h_out.at[index], h_in.at[index], h_send.at[index], h_recv.at[index],
            device_id={"section": section + 1}, device_id_type=MESH,
        )

    def g_copy(index):
        return pltpu.make_async_remote_copy(
            g_out.at[index], g_in.at[index], g_send.at[index], g_recv.at[index],
            device_id={"section": section - 1}, device_id_type=MESH,
        )

    pair_bits = (1, steps - 1)
    half_width = hidden_width // 2

    def active_copy(index, half):
        rows = pl.ds(pl.multiple_of(index * chunk, chunk), chunk)
        columns = slice(half * half_width, (half + 1) * half_width)
        return pltpu.make_async_remote_copy(
            active_all.at[rows, columns], active_far.at[rows, columns],
            active_send.at[index, half], active_recv.at[index, half],
            device_id={"dp": partners[pair_bits[half]]}, device_id_type=MESH,
        )

    def gated_copy(index, half):
        rows = pl.ds(pl.multiple_of(index * chunk, chunk), chunk)
        return pltpu.make_async_remote_copy(
            gated_all.at[rows], gated_far.at[half, rows],
            gated_send.at[index, half], gated_recv.at[index, half],
            device_id={"dp": partners[pair_bits[half]]}, device_id_type=MESH,
        )

    gain_row = gain_ref[...].astype(jnp.float32)
    gain_sum[...] = jnp.zeros_like(gain_sum)
    column_blocks = [slice(at, at + block) for at in range(0, hidden_width, block)]

    def keep_of(index):
        return keep_ref[(index * chunk) // seq_len, section].astype(jnp.float32)

    def forward(index):
        pl.when(section > 0)(lambda: h_copy(index).wait_recv())
        rows = pl.ds(pl.multiple_of(index * chunk, chunk), chunk)
        inputs = h_in[index].astype(jnp.float32)
        inv_rms = lax.rsqrt(jnp.mean(inputs * inputs, axis=-1, keepdims=True) + EPSILON)
        normed = (inputs * inv_rms * gain_row).astype(jnp.bfloat16)
        normed_all[rows, :] = normed
        branch = jnp.zeros((chunk, width), jnp.float32)
        for columns in column_blocks:
            hidden = jnp.dot(normed, w1[:, columns], preferred_element_type=jnp.float32)
            share = 0.5 * (1.0 + lax.erf(hidden * ROOT_HALF))
            active = (hidden * share).astype(jnp.bfloat16)
            active_all[rows, columns] = active
            slope_all[rows, columns] = share + hidden * jnp.exp(-0.5 * hidden * hidden) * DENSITY_SCALE
            branch += lax.dot_general(
                active, w2[:, columns], TRANSPOSED_RHS, preferred_element_type=jnp.float32
            )
        h_out[index] = (inputs + keep_of(index) * branch).astype(jnp.bfloat16)
        h_copy(index).start()
        for half in range(2):
            active_copy(index, half).start()

        @pl.when(index == chunks - 1)
        def _():
            normed_t[...] = normed_all[...].T

    def finish_chunk(index, inputs, inv_rms, upstream, grad_normed):
        @pl.when(section > 0)
        def _():
            scaled = grad_normed * gain_row
            centre = jnp.mean(scaled * inputs, axis=-1, keepdims=True)
            grads = upstream + inv_rms * (scaled - inputs * inv_rms * inv_rms * centre)
            g_out[index] = grads.astype(jnp.bfloat16)
            g_copy(index).start()

        gain_sum[0:1, :] += jnp.sum(grad_normed * inputs * inv_rms, axis=0, keepdims=True)

    def both(index):
        pl.when(section > 0)(lambda: h_copy(index).wait_recv())
        rows = pl.ds(pl.multiple_of(index * chunk, chunk), chunk)
        inputs = h_in[index].astype(jnp.float32)
        inv_rms = lax.rsqrt(jnp.mean(inputs * inputs, axis=-1, keepdims=True) + EPSILON)
        normed = (inputs * inv_rms * gain_row).astype(jnp.bfloat16)
        normed_all[rows, :] = normed
        upstream = g_in[index].astype(jnp.float32)
        gated = gated_all[rows, :]
        grad_normed = jnp.zeros((chunk, width), jnp.float32)
        for columns in column_blocks:
            hidden = jnp.dot(normed, w1[:, columns], preferred_element_type=jnp.float32)
            grad_active = jnp.dot(gated, w2[:, columns], preferred_element_type=jnp.float32)
            share = 0.5 * (1.0 + lax.erf(hidden * ROOT_HALF))
            active_all[rows, columns] = (hidden * share).astype(jnp.bfloat16)
            slope = share + hidden * jnp.exp(-0.5 * hidden * hidden) * DENSITY_SCALE
            grad_hidden = (grad_active * slope).astype(jnp.bfloat16)
            hidden_grad_all[rows, columns] = grad_hidden
            grad_normed += lax.dot_general(
                grad_hidden, w1[:, columns], TRANSPOSED_RHS, preferred_element_type=jnp.float32
            )
        for half in range(2):
            active_copy(index, half).start()
        finish_chunk(index, inputs, inv_rms, upstream, grad_normed)

        @pl.when(index == chunks - 1)
        def _():
            normed_t[...] = normed_all[...].T

    def backward(index):
        g_copy(index).wait_recv()
        rows = pl.ds(pl.multiple_of(index * chunk, chunk), chunk)
        inputs = h_in[index].astype(jnp.float32)
        inv_rms = lax.rsqrt(jnp.mean(inputs * inputs, axis=-1, keepdims=True) + EPSILON)
        upstream = g_in[index].astype(jnp.float32)
        gated = (keep_of(index) * upstream).astype(jnp.bfloat16)
        gated_all[rows, :] = gated
        for half in range(2):
            gated_copy(index, half).start()
        grad_normed = jnp.zeros((chunk, width), jnp.float32)
        for columns in column_blocks:
            grad_active = jnp.dot(gated, w2[:, columns], preferred_element_type=jnp.float32)
            grad_hidden = (grad_active * slope_all[rows, columns]).astype(jnp.bfloat16)
            hidden_grad_all[rows, columns] = grad_hidden
            grad_normed += lax.dot_general(
                grad_hidden, w1[:, columns], TRANSPOSED_RHS, preferred_element_type=jnp.float32
            )
        finish_chunk(index, inputs, inv_rms, upstream, grad_normed)

    pl.when(first)(entry.wait)
    for load in loads:
        load.wait()
    pl.when(last)(cotangents.wait)

    def tick(moment, carry):
        ahead = moment - LAG * section
        behind = moment - LAG * (2 * (sections - 1) - section)
        pl.when(jnp.logical_and(ahead >= 0, ahead < chunks))(lambda: forward(ahead))
        pl.when(jnp.logical_and(behind >= 0, behind < chunks))(lambda: backward(behind))
        return carry

    def send_gated(index, carry):
        rows = pl.ds(pl.multiple_of(index * chunk, chunk), chunk)
        gated_all[rows, :] = (keep_of(index) * g_in[index].astype(jnp.float32)).astype(jnp.bfloat16)
        for half in range(2):
            gated_copy(index, half).start()
        return carry

    def last_tick(index, carry):
        both(index)
        return carry

    @pl.when(last)
    def _():
        lax.fori_loop(0, chunks, send_gated, 0)
        lax.fori_loop(0, chunks, last_tick, 0)

    @pl.when(section < sections - 1)
    def _():
        lax.fori_loop(0, chunks + 2 * LAG * (sections - 1), tick, 0)

    orders_a = (list(range(steps)), [0] + list(range(steps - 1, 0, -1)))
    orders_b = tuple(
        [bit for bit in orders_a[1 - half] if bit != pair_bits[half]] for half in range(2)
    )
    block_rows = width // shards

    def halving(order, parts, landed, send_sem, recv_sem):
        count = 1 << len(order)

        def copy(at, step):
            half = count >> (step + 1)
            bit = order[step]
            source = parts if step == 0 else landed[step - 1]
            return pltpu.make_async_remote_copy(
                source.at[at, pl.ds((1 - bits[bit]) * half, half)],
                landed[step].at[at],
                send_sem.at[at, step],
                recv_sem.at[at, step],
                device_id={"dp": partners[bit]},
                device_id_type=MESH,
            )

        def fill(at, value, places):
            for number, place in enumerate(places):
                rows = value[number * block_rows : (number + 1) * block_rows]
                parts[at, place] = rows.astype(jnp.bfloat16)
            copy(at, 0).start()

        def advance(at, step, finish):
            copy(at, step).wait_recv()
            half = count >> (step + 1)
            source = parts if step == 0 else landed[step - 1]
            own = source[at, pl.ds(bits[order[step]] * half, half)].astype(jnp.float32)
            total = own + landed[step][at].astype(jnp.float32)
            if step + 1 < len(order):
                landed[step][at] = total.astype(jnp.bfloat16)
                copy(at, step + 1).start()
            else:
                finish(total[0])

        def close(at):
            for step in range(len(order)):
                copy(at, step).wait_send()

        return fill, advance, close

    streams_a = [halving(order, parts_a, landed_a, a_send, a_recv) for order in orders_a]
    streams_b = [halving(order, parts_b, landed_b, b_send, b_recv) for order in orders_b]
    fill_g, advance_g, close_g = halving(orders_a[0], parts_g, landed_g, e_send, e_recv)
    gain_lanes = jnp.broadcast_to(gain_sum[0:1, :], (128, width)).T

    def finish_gain(total):
        grad_gain_ref[...] = jnp.transpose(total)[0:1, :]

    def select_features(ref, half, turned):
        bit, order = pair_bits[half], orders_b[half]
        for place in range(shards // 2):
            low = sum(((place >> (len(order) - 1 - k)) & 1) << b for k, b in enumerate(order))
            high = low + (1 << bit)
            pieces = [turned[b * block_rows : (b + 1) * block_rows].astype(jnp.float32) for b in (low, high)]
            chosen = jnp.where(bits[bit] == 1, pieces[1], pieces[0])
            ref[half, place * block_rows : (place + 1) * block_rows] = chosen.astype(jnp.bfloat16)

    def prepare_b():
        def arrive(index, carry):
            for half in range(2):
                active_copy(index, half).wait_recv()
                gated_copy(index, half).wait_recv()
            return carry

        lax.fori_loop(0, chunks, arrive, 0)
        def turn_rows(rows_first):
            return (rows_first if block_rows % 16 == 0 else rows_first.astype(jnp.float32)).T

        turned = turn_rows(gated_all[...])
        for half in range(2):
            select_features(own_t, half, turned)
        for half in range(2):
            select_features(far_t, half, turn_rows(gated_far[half]))

    def columns_of(at, half):
        return pl.ds(pl.multiple_of(at * tile + half * half_width, tile), tile)

    def turn(moment, carry):
        @pl.when(moment < tiles)
        def _():
            for half in range(2):
                value = jnp.dot(
                    normed_t[...],
                    hidden_grad_all[:, columns_of(moment, half)],
                    preferred_element_type=jnp.float32,
                )
                places = [position(b, orders_a[half]) for b in range(shards)]
                streams_a[half][0](half * tiles + moment, value, places)
            pl.when(moment == 0)(prepare_b)
            for half in range(2):
                columns = columns_of(moment, half)
                value = jnp.dot(
                    own_t[half], active_all[:, columns], preferred_element_type=jnp.float32
                ) + jnp.dot(far_t[half], active_far[:, columns], preferred_element_type=jnp.float32)
                streams_b[half][0](half * tiles + moment, value, range(shards // 2))

        for step in range(steps):
            at = moment - (step + 1)

            @pl.when(jnp.logical_and(at >= 0, at < tiles))
            def _(at=at, step=step):
                def finish(out_ref, half):
                    def store(total):
                        out_ref[:, columns_of(at, half)] = total

                    return store

                for half in range(2):
                    streams_a[half][1](half * tiles + at, step, finish(grad_in_ref, half))
                if step + 1 < steps:
                    for half in range(2):
                        streams_b[half][1](half * tiles + at, step, finish(grad_out_ref, half))

            pl.when(moment == step + 2)(lambda step=step: advance_g(0, step, finish_gain))
        return carry

    fill_g(0, gain_lanes, [position(b, orders_a[0]) for b in range(shards)])
    lax.fori_loop(0, max(tiles, 2) + steps, turn, 0)

    def close_chunk(index, carry):
        pl.when(section < sections - 1)(lambda: h_copy(index).wait_send())
        pl.when(section > 0)(lambda: g_copy(index).wait_send())
        for half in range(2):
            active_copy(index, half).wait_send()
            gated_copy(index, half).wait_send()
        return carry

    lax.fori_loop(0, chunks, close_chunk, 0)

    def close_tile(at, carry):
        for half in range(2):
            streams_a[half][2](half * tiles + at)
            streams_b[half][2](half * tiles + at)
        return carry

    lax.fori_loop(0, tiles, close_tile, 0)
    close_g(0)


def per_device(x_in, cotangent, w_in, w_out, gain, drop_mask):
    sections = lax.axis_size("section")
    shards = lax.axis_size("dp")
    micro, micro_rows, width = x_in.shape[1:]
    hidden_width = w_in.shape[2]
    samples, layers = drop_mask.shape[2:]
    seq_len = micro_rows // samples
    rows = micro * micro_rows
    chunk = largest_divisor(seq_len, CHUNK_ROWS, 16)
    chunks = rows // chunk
    block = largest_divisor(hidden_width, HIDDEN_BLOCK, 128)
    tile = largest_divisor(hidden_width // 2, TILE, 128)
    tiles = hidden_width // 2 // tile
    steps = shards.bit_length() - 1
    assert shards == 1 << steps and steps >= 2
    block_rows = width // shards
    dims = (sections, shards, chunk, chunks, seq_len, block, tile, tiles, steps)

    def landing(count, start, columns):
        return [
            pltpu.VMEM((count, shards >> (step + 1), block_rows, columns), jnp.bfloat16)
            for step in range(start, steps)
        ]

    chunk_shape = (chunks, chunk, width)
    any_spec = pl.BlockSpec(memory_space=pl.ANY)
    vmem_spec = pl.BlockSpec(memory_space=pltpu.VMEM)
    dma = pltpu.SemaphoreType.DMA
    macs = 6 * rows * width * hidden_width
    grad_in, grad_out, grad_gain = pl.pallas_call(
        functools.partial(kernel, dims),
        out_shape=(
            jax.ShapeDtypeStruct((block_rows, hidden_width), jnp.float32),
            jax.ShapeDtypeStruct((block_rows, hidden_width), jnp.float32),
            jax.ShapeDtypeStruct((1, block_rows), jnp.float32),
        ),
        in_specs=[pl.BlockSpec(memory_space=pltpu.SMEM), vmem_spec] + [any_spec] * 4,
        out_specs=(vmem_spec,) * 3,
        scratch_shapes=[
            pltpu.VMEM((width, hidden_width), jnp.bfloat16),
            pltpu.VMEM((width, hidden_width), jnp.bfloat16),
            *[pltpu.VMEM(chunk_shape, jnp.bfloat16) for _ in range(4)],
            pltpu.VMEM((rows, width), jnp.bfloat16),
            pltpu.VMEM((rows, width), jnp.bfloat16),
            pltpu.VMEM((rows, hidden_width), jnp.bfloat16),
            pltpu.VMEM((rows, hidden_width), jnp.float32),
            pltpu.VMEM((rows, hidden_width), jnp.bfloat16),
            pltpu.VMEM((8, width), jnp.float32),
            pltpu.VMEM((width, rows), jnp.bfloat16),
            pltpu.VMEM((rows, hidden_width), jnp.bfloat16),
            pltpu.VMEM((2, rows, width), jnp.bfloat16),
            pltpu.VMEM((2, width // 2, rows), jnp.bfloat16),
            pltpu.VMEM((2, width // 2, rows), jnp.bfloat16),
            pltpu.VMEM((2 * tiles, shards, block_rows, tile), jnp.bfloat16),
            pltpu.VMEM((2 * tiles, shards // 2, block_rows, tile), jnp.bfloat16),
            pltpu.VMEM((1, shards, block_rows, 128), jnp.bfloat16),
            *landing(2 * tiles, 0, tile),
            *landing(2 * tiles, 1, tile),
            *landing(1, 0, 128),
            dma((4,)),
            *[dma((chunks,)) for _ in range(4)],
            *[dma((2 * tiles, steps)) for _ in range(4)],
            *[dma((1, steps)) for _ in range(2)],
            *[dma((chunks, 2)) for _ in range(4)],
        ],
        compiler_params=pltpu.CompilerParams(
            collective_id=0, has_side_effects=True, vmem_limit_bytes=62 * 1024 * 1024
        ),
        cost_estimate=pl.CostEstimate(
            flops=2 * macs, bytes_accessed=8 * width * hidden_width, transcendentals=2 * rows * hidden_width
        ),
        name="window",
    )(
        drop_mask[0].reshape(micro * samples, layers),
        gain,
        x_in[0].reshape(chunk_shape),
        cotangent[0].reshape(chunk_shape),
        w_in[0],
        w_out[0],
    )
    return (grad_in[None], grad_out[None], grad_gain)


def solution(mesh):
    placed = (
        P("dp", None, None, None),
        P("dp", None, None, None),
        P("section", None, None),
        P("section", None, None),
        P("section", None),
        P("dp", None, None, None),
    )
    return jax.shard_map(
        per_device,
        mesh=mesh,
        in_specs=placed,
        out_specs=(P("section", "dp", None), P("section", "dp", None), P("section", "dp")),
        check_vma=False,
    )
```
